512 devices in a mesh: dp: 2 (over core), expert: 16 (over z_hi, x), seg: 16 (over z_lo, y).
Axes of the slice: x: 4, y: 4, z: 16 (z_hi: 4, z_lo: 4; z = z_hi * 4 + z_lo), core: 2. Of those that a mesh axis runs over, the one named last changes fastest.
Arguments:
- tokens: bfloat16 [2048, 3072], P(('dp', 'expert'), 'seg'), parts along dimension 0, may hold values from -6 to 6
- expert_ids: int32 [2048, 4], P(('dp', 'expert')), parts along dimension 0, may hold values from 0 to 15, as said below
- route_weight: float32 [2048, 4], P(('dp', 'expert')), parts along dimension 0, may hold values from 0.1 to 1
- w_up: bfloat16 [16, 3072, 6144], P('expert', None, 'seg'), may hold values from -0.109375 to 0.109375
- w_down: bfloat16 [16, 6144, 3072], P('expert', 'seg'), may hold values from -0.078125 to 0.078125
Outputs:
- mixed: bfloat16 [2048, 3072], P(('dp', 'expert'), 'seg'), parts along dimension 0
The draws below stay inside these ranges and needn't reach their ends.
There are 2 independent parts, one for each index of `dp`. The reference program is written for one: setup_inputs(seed, part) draws one part's arguments, and reference() takes and returns one part's arrays. A program takes and returns all parts, laid end to end along the dimension named above; an argument that names none is the same for every part. Nothing has to cross between parts.
Inputs may be any that keep to these rules, and one draw needn't show every extreme that they name: `expert_ids`: each row names 4 different experts. Within each aligned block of 64 rows (the rows of one device), no expert is named by more than 21 rows, and one expert is named by exactly 21 rows in every block.
All inputs are finite; a program needn't handle non-finite values.
Results may differ from the reference program's by a relative error of at most 0.0049.
Values may be sent and summed in bfloat16 or wider, within the bound.
A program may use at most 64 MiB of HBM per device.

```python
import math
import jax
import jax.numpy as jnp
from jax import lax

D = 3072
FF = 6144
EXPERTS = 16
TOPK = 4
TOK_DEV = 64
SEND_CAP = 21
TOKENS = 1024


def draw_expert_ids(key, part):
    blocks = TOKENS // TOK_DEV
    key_hot, key_rows = jax.random.split(jax.random.fold_in(key, 11), 2)
    hottest = jax.random.randint(key_hot, (), 0, EXPERTS)
    column = jnp.arange(TOPK, dtype=jnp.int32)[None, :]

    def one_block(block_key):
        key_first, key_second, key_third = jax.random.split(block_key, 3)
        chosen = jax.random.permutation(key_first, TOK_DEV)
        has_hot = jnp.zeros((TOK_DEV,), jnp.int32).at[chosen[:SEND_CAP]].set(1)
        others = TOPK - has_hot
        offset = jnp.cumsum(others) - others
        order = jax.random.permutation(key_second, EXPERTS - 1)
        picks = order[(offset[:, None] + column) % (EXPERTS - 1)]
        picks = picks + (picks >= hottest).astype(jnp.int32)
        shifted = jnp.concatenate([jnp.full((TOK_DEV, 1), hottest, jnp.int32), picks[:, :TOPK - 1]], axis=1)
        chosen_rows = jnp.where(has_hot[:, None] == 1, shifted, picks)
        turned = jax.random.randint(key_third, (TOK_DEV, 1), 0, TOPK)
        return jnp.take_along_axis(chosen_rows, (column + turned) % TOPK, axis=1)
    keys = jax.random.split(key_rows, blocks)
    return jax.vmap(one_block)(keys).reshape(TOKENS, TOPK).astype(jnp.int32)


def steps_of(stream_key, extent, cuts, low, largest):
    def one(axis_at, parts):
        draws = jax.random.uniform(jax.random.fold_in(jax.random.fold_in(stream_key, 6), axis_at), (parts,), jnp.float32, low / len(cuts), largest / len(cuts))
        return jnp.repeat(jnp.exp(draws), extent[axis_at] // parts).reshape((-1,) + (1,) * (len(extent) - axis_at - 1))

    loudness = one(*cuts[0])
    for cut in cuts[1:]:
        loudness = loudness * one(*cut)
    return loudness


def bell_draw(key, dims, width, reach, shards=(), kind=jnp.bfloat16):
    gain = steps_of(key, dims, shards, -0.22, 0.18) if shards else 1.0
    drawn = jax.random.normal(key, dims, jnp.float32) * width * gain
    return jnp.minimum(jnp.maximum(drawn, -reach), reach).astype(kind)


def setup_inputs(seed: int = 0, part: int = 0) -> dict:
    splits = jax.random.split(jax.random.key(seed), 6)
    part_splits = jax.random.split(jax.random.fold_in(splits[5], part), 6)
    return {
        "tokens": bell_draw(part_splits[0], (TOKENS, D), 1.0, 6.0, ((0, 16), (1, 16))),
        "expert_ids": draw_expert_ids(jax.random.fold_in(jax.random.fold_in(splits[5], part), 71), part),
        "route_weight": jnp.clip(jnp.exp(math.log(1.0) - 2.3025851 * jax.random.uniform(part_splits[2], (TOKENS, TOPK), jnp.float32) ** steps_of(part_splits[2], (TOKENS, TOPK), ((0, 16),), -0.2, 0.2)), 0.1, 1.0),
        "w_up": bell_draw(splits[3], (EXPERTS, D, FF), D ** -0.5, 0.109375, ((0, 16), (2, 16))),
        "w_down": bell_draw(splits[4], (EXPERTS, FF, D), FF ** -0.5, 0.078125, ((0, 16), (1, 16))),
    }


def reference(tokens, expert_ids, route_weight, w_up, w_down):
    tok_all = tokens.shape[0]
    topk = expert_ids.shape[1]
    blocks = tok_all // TOK_DEV
    grouped = expert_ids.reshape(blocks, TOK_DEV * topk)
    onehot = (grouped[:, :, None] == jnp.arange(EXPERTS, dtype=jnp.int32)[None, None, :]).astype(jnp.int32)
    before = jnp.cumsum(onehot, axis=1) - onehot
    slot = jnp.sum(before * onehot, axis=2)
    source = jnp.arange(blocks, dtype=jnp.int32)[:, None]
    dest = (source * SEND_CAP + slot).reshape(-1).astype(jnp.int32)
    flat_route = expert_ids.reshape(-1)
    repeated = jnp.repeat(tokens, topk, axis=0)
    norm_weight = route_weight / jnp.sum(route_weight, axis=1, keepdims=True)
    flat_weight = norm_weight.reshape(-1)
    cap_rows = blocks * SEND_CAP

    def one_expert(total, inputs):
        expert, up_weight, down_weight = inputs
        mine = flat_route == expert
        index = jnp.where(mine, dest, cap_rows).astype(jnp.int32)
        buffer = jnp.zeros((cap_rows, tokens.shape[1]), jnp.bfloat16).at[index].set(repeated, mode="drop")
        up_sum = jnp.dot(buffer, up_weight, preferred_element_type=jnp.float32)
        hidden = jax.nn.silu(up_sum).astype(jnp.bfloat16)
        result = jnp.dot(hidden, down_weight, preferred_element_type=jnp.float32)
        picked = result[jnp.minimum(index, cap_rows - 1)]
        factor = jnp.where(mine, flat_weight, jnp.zeros_like(flat_weight))
        return total + picked * factor[:, None], None

    start = jnp.zeros((tok_all * topk, tokens.shape[1]), jnp.float32)
    total, _ = lax.scan(one_expert, start, (jnp.arange(EXPERTS, dtype=jnp.int32), w_up, w_down))
    return total.reshape(tok_all, topk, tokens.shape[1]).sum(axis=1).astype(jnp.bfloat16)
```

```python
import functools

import jax
import jax.numpy as jnp
from jax import lax
from jax.experimental import pallas as pl
from jax.experimental.pallas import tpu as pltpu
from jax.sharding import PartitionSpec as P

CAP = 21
PACK = 32
LANES = 128
SIDE = 4
F32 = jnp.float32
BF16 = jnp.bfloat16


def mm(a, b):
    return jnp.dot(a, b, preferred_element_type=F32)


def mm_t(a, b):
    return lax.dot_general(a, b, (((0,), (0,)), ((), ())), preferred_element_type=F32)


def layer(
    experts, tok_ref, ids_ref, rw_ref, wup_ref, wdn_ref, out_ref,
    sbuf, ag, wu, wraw, wd, acc, hp, a_up, a_dn, b_up, b_dn, ra_up, ra_dn, rb_up, rb_dn,
    keep_up, keep_dn, own, zs, zr, fbuf, rbuf,
    wsem, d_s, d_r, z_s, z_r, y_s, y_r, r_s, r_r, zz_s, zz_r, t_s, t_r,
):
    topk = ids_ref.shape[1]
    tokens = tok_ref.shape[0]
    rows = experts * PACK
    half = rows // 2
    width = wup_ref.shape[2]
    e = lax.axis_index("expert")
    s = lax.axis_index("seg")
    zl, y = s // SIDE, s % SIDE
    up = (y + 1) % SIDE
    down = (y + SIDE - 1) % SIDE
    far = (y + 2) % SIDE
    zpeer = [zl, zl + 1 - 2 * (zl % 2), (zl + 2) % SIDE, SIDE - 1 - zl]
    seg_up, seg_down = zl * SIDE + up, zl * SIDE + down

    barrier = pltpu.get_barrier_semaphore()

    def greet(i, c):
        pl.semaphore_signal(barrier, inc=1, device_id={"expert": (e + i) % experts})
        return c

    lax.fori_loop(1, experts, greet, 0)
    for to in (seg_up, seg_down, *[zpeer[j] * SIDE + y for j in range(1, SIDE)]):
        pl.semaphore_signal(barrier, inc=1, device_id={"seg": to})

    loads = [
        pltpu.make_async_copy(wup_ref.at[:, 0:128, :], wu.at[:, :, 0:width], wsem.at[0]),
        pltpu.make_async_copy(wup_ref.at[:, 128:192, :], wu.at[:, 0:64, width : 2 * width], wsem.at[1]),
        pltpu.make_async_copy(wup_ref.at[:, 128:192, :], wu.at[:, 64:128, 2 * width : 3 * width], wsem.at[2]),
        pltpu.make_async_copy(wdn_ref, wraw, wsem.at[3]),
    ]
    for c in loads:
        c.start()

    lane = lax.broadcasted_iota(jnp.int32, (tokens, rows), 1)
    lane_e, lane_r = lane // PACK, lane % PACK
    ids = ids_ref[...]
    rw = rw_ref[...]
    norm = rw / jnp.sum(rw, axis=1, keepdims=True)
    weight = jnp.zeros((tokens, rows), F32)
    named = jnp.zeros((tokens, rows), F32)
    for k in range(topk):
        hit = ids[:, k : k + 1] == lane_e
        named = jnp.where(hit, 1.0, named)
        weight = jnp.where(hit, norm[:, k : k + 1], weight)
    earlier = lax.broadcasted_iota(jnp.int32, (tokens, tokens), 1) < lax.broadcasted_iota(
        jnp.int32, (tokens, tokens), 0
    )
    slot = mm(jnp.where(earlier, 1.0, 0.0).astype(BF16), named.astype(BF16)).astype(jnp.int32)
    main = lane_r < CAP
    place = jnp.concatenate(
        [
            jnp.where(main & (slot == lane_r), named, 0.0),
            jnp.where(~main & (slot == lane_r - CAP), named, 0.0),
            jnp.where(~main & (slot == lane_r - 10), named, 0.0),
        ],
        axis=0,
    )
    tok = tok_ref[...]
    rest = tok[:, 128:192].astype(F32)
    blank = jnp.zeros((tokens, 64), F32)
    source = jnp.concatenate(
        [
            tok[:, 0:128],
            jnp.concatenate([rest, blank], axis=1).astype(BF16),
            jnp.concatenate([blank, rest], axis=1).astype(BF16),
        ],
        axis=0,
    )
    sbuf[...] = mm_t(place.astype(BF16), source).astype(BF16)

    pl.semaphore_wait(barrier, experts - 1 + SIDE + 1)

    def dispatch(i):
        to = (e + i) % experts
        return pltpu.make_async_remote_copy(
            src_ref=sbuf.at[pl.ds(to * PACK, PACK)],
            dst_ref=ag.at[s, pl.ds(e * PACK, PACK)],
            send_sem=d_s.at[i],
            recv_sem=d_r.at[i],
            device_id={"expert": to},
        )

    def start_dispatch(i, c):
        dispatch(i).start()
        return c

    lax.fori_loop(1, experts, start_dispatch, 0)
    ag[s, pl.ds(e * PACK, PACK), :] = sbuf[pl.ds(e * PACK, PACK), :]

    wu[:, 64:128, width : 2 * width] = jnp.zeros((wu.shape[0], 64, width), BF16)
    wu[:, 0:64, 2 * width : 3 * width] = jnp.zeros((wu.shape[0], 64, width), BF16)
    loads[3].wait()
    left = lax.broadcasted_iota(jnp.int32, (width, LANES), 1) < 64

    def pad_down(i, c):
        z, q = i // 2, i % 2
        base = pl.multiple_of(i * 384, 128)
        a = wraw[:, pl.ds(base, 128)]
        b = wraw[:, pl.ds(base + 128, 128)].astype(F32)
        g = wraw[:, pl.ds(base + 256, 128)].astype(F32)
        b_turn, g_turn = pltpu.roll(b, 64, 1), pltpu.roll(g, 64, 1)
        to0 = pl.multiple_of((2 * q + 6 - y) % SIDE * LANES, LANES)
        to1 = pl.multiple_of((2 * q + 7 - y) % SIDE * LANES, LANES)
        wd[z, 0:width, pl.ds(to0, LANES)] = a
        wd[z, width : 2 * width, pl.ds(to0, LANES)] = jnp.where(left, b, 0.0).astype(BF16)
        wd[z, 2 * width : 3 * width, pl.ds(to0, LANES)] = jnp.where(left, 0.0, b_turn).astype(BF16)
        wd[z, 0:width, pl.ds(to1, LANES)] = jnp.where(left, b_turn, g_turn).astype(BF16)
        wd[z, width : 2 * width, pl.ds(to1, LANES)] = jnp.where(left, g_turn, 0.0).astype(BF16)
        wd[z, 2 * width : 3 * width, pl.ds(to1, LANES)] = jnp.where(left, 0.0, g).astype(BF16)
        return c

    lax.fori_loop(0, 2 * SIDE, pad_down, 0)
    for c in loads[:3]:
        c.wait()

    def wait_dispatch(i, c):
        dispatch(i).wait_recv()
        return c

    lax.fori_loop(1, experts, wait_dispatch, 0)

    def zcopy(j):
        return pltpu.make_async_remote_copy(
            src_ref=ag.at[s],
            dst_ref=ag.at[s],
            send_sem=z_s.at[j],
            recv_sem=z_r.at[j],
            device_id={"seg": zpeer[j] * SIDE + y},
        )

    def z_arrival(j):
        g = zpeer[j] * SIDE + y
        return pltpu.make_async_remote_copy(
            src_ref=ag.at[g], dst_ref=ag.at[g], send_sem=z_s.at[j], recv_sem=z_r.at[j], device_id={"seg": g}
        )

    lo, hi = pl.ds(0, half), pl.ds(half, half)

    def ycopy(j, line, col, part, to):
        g = zpeer[j] * SIDE + col
        return pltpu.make_async_remote_copy(
            src_ref=ag.at[g, part],
            dst_ref=ag.at[g, part],
            send_sem=y_s.at[j, line],
            recv_sem=y_r.at[j, line],
            device_id={"seg": to},
        )

    def y_send(j):
        for c in (
            ycopy(j, 0, y, lo, seg_up),
            ycopy(j, 1, y, hi, seg_down),
            ycopy(j, 2, y, hi, seg_up),
            ycopy(j, 3, y, lo, seg_down),
        ):
            c.start()

    def y_pass(j):
        ycopy(j, 0, down, lo, seg_up).wait_recv()
        ycopy(j, 4, down, lo, seg_up).start()
        ycopy(j, 1, up, hi, seg_down).wait_recv()
        ycopy(j, 5, up, hi, seg_down).start()

    def up_part(j, first):
        ycopy(j, 2, down, hi, seg_up).wait_recv()
        ycopy(j, 3, up, lo, seg_down).wait_recv()
        ycopy(j, 4, far, lo, seg_up).wait_recv()
        ycopy(j, 5, far, hi, seg_down).wait_recv()
        g = zpeer[j] * SIDE
        x = jnp.concatenate([ag[g + i] for i in range(SIDE)], axis=1)
        w = wu[pl.ds(g, SIDE)].reshape(SIDE * LANES, 3 * width)
        if first:
            acc[...] = mm(x, w)
        else:
            acc[...] += mm(x, w)

    for j in range(1, SIDE):
        zcopy(j).start()
    y_send(0)
    for j in range(1, SIDE):
        z_arrival(j).wait_recv()
        y_send(j)
        y_pass(j - 1)
        if j > 1:
            up_part(j - 2, j == 2)
    y_pass(SIDE - 1)
    up_part(SIDE - 2, False)
    up_part(SIDE - 1, False)

    r = lax.broadcasted_iota(jnp.int32, (rows, width), 0) % PACK
    spread = jnp.where(
        r < 11,
        pltpu.roll(acc[:, width : 2 * width], rows - 21, 0),
        pltpu.roll(acc[:, 2 * width : 3 * width], rows - 10, 0),
    )
    v = acc[:, 0:width] + spread
    h = jnp.where(r < CAP, v / (1.0 + jnp.exp(-v)), 0.0)
    hp[:, 0:width] = h.astype(BF16)
    hp[:, width : 2 * width] = jnp.where(r < CAP, 0.0, pltpu.roll(h, 21, 0)).astype(BF16)
    hp[:, 2 * width : 3 * width] = jnp.where(r < CAP, 0.0, pltpu.roll(h, 10, 0)).astype(BF16)

    def rcopy(j, line, src, dst, to):
        return pltpu.make_async_remote_copy(
            src_ref=src,
            dst_ref=dst,
            send_sem=r_s.at[j, line],
            recv_sem=r_r.at[j, line],
            device_id={"seg": to},
        )

    def line(j, n):
        return (
            lambda: rcopy(j, 0, a_up.at[j], ra_up.at[j], seg_up),
            lambda: rcopy(j, 1, a_dn.at[j], ra_dn.at[j], seg_down),
            lambda: rcopy(j, 2, b_up.at[j, hi], rb_up.at[j, hi], seg_up),
            lambda: rcopy(j, 3, b_dn.at[j, lo], rb_dn.at[j, lo], seg_down),
            lambda: rcopy(j, 4, b_up.at[j, lo], rb_up.at[j, lo], seg_up),
            lambda: rcopy(j, 5, b_dn.at[j, hi], rb_dn.at[j, hi], seg_down),
        )[n]()

    def down_first(j):
        part = mm(hp[...], wd[zpeer[j]])
        a_up[j] = part[0:half, 0:128].astype(BF16)
        a_dn[j] = part[half:rows, 0:128].astype(BF16)
        line(j, 0).start()
        line(j, 1).start()
        b_up[j, half:rows] = part[half:rows, 384:512].astype(BF16)
        b_dn[j, 0:half] = part[0:half, 128:256].astype(BF16)
        line(j, 2).start()
        line(j, 3).start()
        keep_up[j] = part[0:half, 384:512]
        keep_dn[j] = part[half:rows, 128:256]
        own[j] = part[:, 256:384]

    def down_second(j):
        line(j, 0).wait_recv()
        b_up[j, 0:half] = (keep_up[j] + ra_up[j].astype(F32)).astype(BF16)
        line(j, 4).start()
        line(j, 1).wait_recv()
        b_dn[j, half:rows] = (keep_dn[j] + ra_dn[j].astype(F32)).astype(BF16)
        line(j, 5).start()

    def zsum(j):
        return pltpu.make_async_remote_copy(
            src_ref=zs.at[j],
            dst_ref=zr.at[j],
            send_sem=zz_s.at[j],
            recv_sem=zz_r.at[j],
            device_id={"seg": zpeer[j] * SIDE + y},
        )

    def down_third(j):
        for n in range(2, 6):
            line(j, n).wait_recv()
        total = own[j] + rb_up[j].astype(F32) + rb_dn[j].astype(F32)
        if j:
            zs[j] = total.astype(BF16)
            zsum(j).start()
        else:
            own[j] = total

    down_first(1)
    down_first(2)
    down_second(1)
    down_first(3)
    down_second(2)
    down_third(1)
    down_first(0)
    down_second(3)
    down_third(2)
    down_second(0)
    down_third(3)
    down_third(0)
    total = own[0]
    for j in range(1, SIDE):
        zsum(j).wait_recv()
        total += zr[j].astype(F32)
    fbuf[...] = total.astype(BF16)

    def back(i):
        to = (e + i) % experts
        return pltpu.make_async_remote_copy(
            src_ref=fbuf.at[pl.ds(to * PACK, PACK)],
            dst_ref=rbuf.at[pl.ds(e * PACK, PACK)],
            send_sem=t_s.at[i],
            recv_sem=t_r.at[i],
            device_id={"expert": to},
        )

    def start_back(i, c):
        back(i).start()
        return c

    lax.fori_loop(1, experts, start_back, 0)
    rbuf[pl.ds(e * PACK, PACK), :] = fbuf[pl.ds(e * PACK, PACK), :]
    scaled = place * jnp.concatenate([weight] * 3, axis=0)
    big = scaled.astype(BF16)
    small = (scaled - big.astype(F32)).astype(BF16)

    for j in range(SIDE):
        if j:
            zcopy(j).wait_send()
            zsum(j).wait_send()
        ycopy(j, 0, y, lo, seg_up).wait_send()
        ycopy(j, 1, y, hi, seg_down).wait_send()
        ycopy(j, 2, y, hi, seg_up).wait_send()
        ycopy(j, 3, y, lo, seg_down).wait_send()
        ycopy(j, 4, down, lo, seg_up).wait_send()
        ycopy(j, 5, up, hi, seg_down).wait_send()
        for n in range(6):
            line(j, n).wait_send()

    def wait_sent(i, c):
        dispatch(i).wait_send()
        back(i).wait_send()
        return c

    lax.fori_loop(1, experts, wait_sent, 0)

    def wait_back(i, c):
        back(i).wait_recv()
        return c

    lax.fori_loop(1, experts, wait_back, 0)
    got = rbuf[...]
    mixed = mm(big, got) + mm(small, got)
    out_ref[:, 0:128] = mixed[0:tokens].astype(BF16)
    tail = mixed[tokens : 2 * tokens, 0:64] + mixed[2 * tokens : 3 * tokens, 64:128]
    out_ref[:, 128:192] = tail.astype(BF16)


def shards(experts, tokens, expert_ids, route_weight, w_up, w_down):
    segs = SIDE * SIDE
    rows = experts * PACK
    half = rows // 2
    width = w_up.shape[2]
    block = tokens.shape[1]
    vm = pltpu.VMEM
    dma = pltpu.SemaphoreType.DMA
    return pl.pallas_call(
        functools.partial(layer, experts),
        out_shape=jax.ShapeDtypeStruct(tokens.shape, BF16),
        in_specs=[pl.BlockSpec(memory_space=vm)] * 3 + [pl.BlockSpec(memory_space=pl.ANY)] * 2,
        out_specs=pl.BlockSpec(memory_space=vm),
        scratch_shapes=[
            vm((rows, LANES), BF16),
            vm((segs, rows, LANES), BF16),
            vm((segs, LANES, 3 * width), BF16),
            vm((width, segs * block), BF16),
            vm((SIDE, 3 * width, SIDE * LANES), BF16),
            vm((rows, 3 * width), F32),
            vm((rows, 3 * width), BF16),
            vm((SIDE, half, LANES), BF16),
            vm((SIDE, half, LANES), BF16),
            vm((SIDE, rows, LANES), BF16),
            vm((SIDE, rows, LANES), BF16),
            vm((SIDE, half, LANES), BF16),
            vm((SIDE, half, LANES), BF16),
            vm((SIDE, rows, LANES), BF16),
            vm((SIDE, rows, LANES), BF16),
            vm((SIDE, half, LANES), F32),
            vm((SIDE, half, LANES), F32),
            vm((SIDE, rows, LANES), F32),
            vm((SIDE, rows, LANES), BF16),
            vm((SIDE, rows, LANES), BF16),
            vm((rows, LANES), BF16),
            vm((rows, LANES), BF16),
            dma((4,)),
            dma((experts,)),
            dma((experts,)),
            dma((SIDE,)),
            dma((SIDE,)),
            dma((SIDE, 6)),
            dma((SIDE, 6)),
            dma((SIDE, 6)),
            dma((SIDE, 6)),
            dma((SIDE,)),
            dma((SIDE,)),
            dma((experts,)),
            dma((experts,)),
        ],
        compiler_params=pltpu.CompilerParams(
            collective_id=0, has_side_effects=True, vmem_limit_bytes=56 * 2**20
        ),
    )(
        tokens,
        expert_ids,
        route_weight,
        w_up.reshape(segs, block, width),
        w_down.reshape(width, segs * block),
    )


def solution(mesh):
    placed = (
        P(("dp", "expert"), "seg"),
        P(("dp", "expert"), None),
        P(("dp", "expert"), None),
        P("expert", None, "seg"),
        P("expert", "seg", None),
    )
    return jax.shard_map(
        functools.partial(shards, mesh.shape["expert"]),
        mesh=mesh,
        in_specs=placed,
        out_specs=P(("dp", "expert"), "seg"),
        check_vma=False,
    )
```

```python
import functools

import jax
import jax.numpy as jnp
from jax import lax
from jax.experimental import pallas as pl
from jax.experimental.pallas import tpu as pltpu
from jax.sharding import PartitionSpec as P

CAP = 21
PACK = 32
LANES = 128
SIDE = 4
OFF = (0, 1, 3, 2)
LAG2, LAG3, LAG4 = 3, 6, 3
F32 = jnp.float32
BF16 = jnp.bfloat16


def mm(a, b):
    return jnp.dot(a, b, preferred_element_type=F32)


def mm_t(a, b):
    return lax.dot_general(a, b, (((0,), (0,)), ((), ())), preferred_element_type=F32)


def layer(
    experts, tok_ref, ids_ref, rw_ref, wup_ref, wdn_ref, out_ref,
    sbuf, mid, ag, wu, wraw, wd, hp, place, a_up, a_dn, b_up, b_dn, ra_up, ra_dn, rb_up, rb_dn,
    keep_up, keep_dn, own, zs, zr, fb, rb1, rb2,
    wsem, dx_s, dx_r, dz_s, dz_r, z_s, z_r, y_s, y_r, r_s, r_r, zz_s, zz_r, th_s, th_r, tx_s, tx_r,
):
    topk = ids_ref.shape[0]
    tokens = tok_ref.shape[0]
    xs = experts // SIDE
    chunk = xs * PACK
    half = chunk // 2
    rows = SIDE * chunk
    width = wup_ref.shape[2]
    e = lax.axis_index("expert")
    s = lax.axis_index("seg")
    zh, x = e // xs, e % xs
    zl, y = s // SIDE, s % SIDE
    up = (y + 1) % SIDE
    down = (y + SIDE - 1) % SIDE
    far = (y + 2) % SIDE
    zpeer = [zl, zl + 1 - 2 * (zl % 2), (zl + 2) % SIDE, SIDE - 1 - zl]
    seg_up, seg_down = zl * SIDE + up, zl * SIDE + down

    def at_zh(off):
        return {"expert": (zh + SIDE + off) % SIDE * xs + x}

    def at_x(i):
        return {"expert": zh * xs + (x + i) % xs}

    barrier = pltpu.get_barrier_semaphore()
    near = [at_x(i) for i in range(1, xs)] + [at_zh(1), at_zh(-1)]
    near += [{"seg": seg_up}, {"seg": seg_down}]
    near += [{"seg": zpeer[j] * SIDE + y} for j in range(1, SIDE)]
    for to in near:
        pl.semaphore_signal(barrier, inc=1, device_id=to)

    loads = [
        pltpu.make_async_copy(wup_ref.at[:, 0:128, :], wu.at[:, :, 0:width], wsem.at[0]),
        pltpu.make_async_copy(wup_ref.at[:, 128:192, :], wu.at[:, 0:64, width : 2 * width], wsem.at[1]),
        pltpu.make_async_copy(wup_ref.at[:, 128:192, :], wu.at[:, 64:128, 2 * width : 3 * width], wsem.at[2]),
        pltpu.make_async_copy(wdn_ref, wraw, wsem.at[3]),
    ]
    for c in loads:
        c.start()

    table = jnp.concatenate([ids_ref[...].astype(F32), rw_ref[...]], axis=0).T
    ids, rw = table[:, 0:topk], table[:, topk : 2 * topk]
    norm = rw / jnp.sum(rw, axis=1, keepdims=True)
    lane = lax.broadcasted_iota(jnp.int32, (tokens, rows), 1)
    lane_c, lane_x, lane_r = lane // chunk, lane % chunk // PACK, lane % PACK
    lane_off = jnp.where(lane_c == 0, 0, jnp.where(lane_c == 1, 1, 5 - lane_c))
    lane_e = ((zh + SIDE - lane_off) % SIDE * xs + lane_x).astype(F32)
    weight = jnp.zeros((tokens, rows), F32)
    named = jnp.zeros((tokens, rows), F32)
    for k in range(topk):
        hit = ids[:, k : k + 1] == lane_e
        named = jnp.where(hit, 1.0, named)
        weight = jnp.where(hit, norm[:, k : k + 1], weight)
    earlier = lax.broadcasted_iota(jnp.int32, (tokens, tokens), 1) < lax.broadcasted_iota(
        jnp.int32, (tokens, tokens), 0
    )
    slot = mm(jnp.where(earlier, 1.0, 0.0).astype(BF16), named.astype(BF16)).astype(jnp.int32)
    main = lane_r < CAP
    puts = (main & (slot == lane_r), ~main & (slot == lane_r - CAP), ~main & (slot == lane_r - 10))
    tok = tok_ref[...]
    rest = tok[:, 128:192].astype(F32)
    blank = jnp.zeros((tokens, 64), F32)
    source = jnp.concatenate(
        [
            tok[:, 0:128],
            jnp.concatenate([rest, blank], axis=1).astype(BF16),
            jnp.concatenate([blank, rest], axis=1).astype(BF16),
        ],
        axis=0,
    )
    onehot = jnp.concatenate([jnp.where(p, named, 0.0) for p in puts], axis=0)
    sbuf[...] = mm_t(onehot.astype(BF16), source).astype(BF16).reshape(SIDE, chunk, LANES)

    pl.semaphore_wait(barrier, len(near))

    def first_x(i):
        to = (x + i) % xs
        return pltpu.make_async_remote_copy(
            src_ref=sbuf.at[0, pl.ds(to * PACK, PACK)],
            dst_ref=ag.at[0, s, pl.ds(x * PACK, PACK)],
            send_sem=dx_s.at[0, i],
            recv_sem=dx_r.at[0, i],
            device_id=at_x(i),
        )

    def other_x(i):
        to = (x + i) % xs
        return pltpu.make_async_remote_copy(
            src_ref=sbuf.at[pl.ds(1, SIDE - 1), pl.ds(to * PACK, PACK)],
            dst_ref=mid.at[:, pl.ds(x * PACK, PACK)],
            send_sem=dx_s.at[1, i],
            recv_sem=dx_r.at[1, i],
            device_id=at_x(i),
        )

    def across(c):
        return pltpu.make_async_remote_copy(
            src_ref=mid.at[c - 1],
            dst_ref=ag.at[c, s],
            send_sem=dz_s.at[c],
            recv_sem=dz_r.at[c],
            device_id=at_zh(-OFF[c]),
        )

    for i in range(1, xs):
        first_x(i).start()
    for i in range(1, xs):
        other_x(i).start()
    mine = pl.ds(x * PACK, PACK)
    ag[0, s, mine, :] = sbuf[0, mine, :]
    for c in range(1, SIDE):
        mid[c - 1, mine, :] = sbuf[c, mine, :]

    def zcopy(c, j):
        return pltpu.make_async_remote_copy(
            src_ref=ag.at[c, s],
            dst_ref=ag.at[c, s],
            send_sem=z_s.at[c, j],
            recv_sem=z_r.at[c, j],
            device_id={"seg": zpeer[j] * SIDE + y},
        )

    def z_arrival(c, j):
        g = zpeer[j] * SIDE + y
        return pltpu.make_async_remote_copy(
            src_ref=ag.at[c, g],
            dst_ref=ag.at[c, g],
            send_sem=z_s.at[c, j],
            recv_sem=z_r.at[c, j],
            device_id={"seg": g},
        )

    def ycopy(c, j, line):
        col, part, to = (
            (y, pl.ds(0, chunk), seg_up),
            (y, pl.ds(0, chunk), seg_down),
            (down, pl.ds(0, half), seg_up),
            (up, pl.ds(half, half), seg_down),
        )[line]
        g = zpeer[j] * SIDE + col
        return pltpu.make_async_remote_copy(
            src_ref=ag.at[c, g, part],
            dst_ref=ag.at[c, g, part],
            send_sem=y_s.at[c, j, line],
            recv_sem=y_r.at[c, j, line],
            device_id={"seg": to},
        )

    def y_arrival(c, j, line):
        col, part = (
            (down, pl.ds(0, chunk)),
            (up, pl.ds(0, chunk)),
            (far, pl.ds(0, half)),
            (far, pl.ds(half, half)),
        )[line]
        g = zpeer[j] * SIDE + col
        return pltpu.make_async_remote_copy(
            src_ref=ag.at[c, g, part],
            dst_ref=ag.at[c, g, part],
            send_sem=y_s.at[c, j, line],
            recv_sem=y_r.at[c, j, line],
            device_id={"seg": seg_up},
        )

    def y_send(c, j):
        ycopy(c, j, 0).start()
        ycopy(c, j, 1).start()

    def own_out(c):
        for j in range(1, SIDE):
            zcopy(c, j).start()
        y_send(c, 0)

    def z_out(c):
        for j in range(1, SIDE):
            z_arrival(c, j).wait_recv()
            y_send(c, j)

    def y_pass(c):
        for j in range(SIDE):
            y_arrival(c, j, 0).wait_recv()
            ycopy(c, j, 2).start()
            y_arrival(c, j, 1).wait_recv()
            ycopy(c, j, 3).start()

    r = lax.broadcasted_iota(jnp.int32, (chunk, width), 0) % PACK

    def up_part(c):
        for j in range(SIDE):
            y_arrival(c, j, 2).wait_recv()
            y_arrival(c, j, 3).wait_recv()
        lhs = jnp.concatenate([ag[c, g] for g in range(SIDE * SIDE)], axis=1)
        u = mm(lhs, wu[...].reshape(SIDE * SIDE * LANES, 3 * width))
        v = u[:, 0:width] + jnp.where(
            r < 11,
            pltpu.roll(u[:, width : 2 * width], chunk - 21, 0),
            pltpu.roll(u[:, 2 * width : 3 * width], chunk - 10, 0),
        )
        h = jnp.where(r < CAP, v / (1.0 + jnp.exp(-v)), 0.0)
        hp[c, :, 0:width] = h.astype(BF16)
        hp[c, :, width : 2 * width] = jnp.where(r < CAP, 0.0, pltpu.roll(h, 21, 0)).astype(BF16)
        hp[c, :, 2 * width : 3 * width] = jnp.where(r < CAP, 0.0, pltpu.roll(h, 10, 0)).astype(BF16)

    left = lax.broadcasted_iota(jnp.int32, (width, LANES), 1) < 64

    def pad_down(i, c):
        z, q = i // 2, i % 2
        base = pl.multiple_of(i * 384, 128)
        a = wraw[:, pl.ds(base, 128)]
        b = wraw[:, pl.ds(base + 128, 128)].astype(F32)
        g = wraw[:, pl.ds(base + 256, 128)].astype(F32)
        b_turn, g_turn = pltpu.roll(b, 64, 1), pltpu.roll(g, 64, 1)
        to0 = pl.multiple_of((2 * q + 6 - y) % SIDE * LANES, LANES)
        to1 = pl.multiple_of((2 * q + 7 - y) % SIDE * LANES, LANES)
        wd[z, 0:width, pl.ds(to0, LANES)] = a
        wd[z, width : 2 * width, pl.ds(to0, LANES)] = jnp.where(left, b, 0.0).astype(BF16)
        wd[z, 2 * width : 3 * width, pl.ds(to0, LANES)] = jnp.where(left, 0.0, b_turn).astype(BF16)
        wd[z, 0:width, pl.ds(to1, LANES)] = jnp.where(left, b_turn, g_turn).astype(BF16)
        wd[z, width : 2 * width, pl.ds(to1, LANES)] = jnp.where(left, g_turn, 0.0).astype(BF16)
        wd[z, 2 * width : 3 * width, pl.ds(to1, LANES)] = jnp.where(left, 0.0, g).astype(BF16)
        return c

    for i in range(1, xs):
        first_x(i).wait_recv()
    own_out(0)
    for i in range(1, xs):
        other_x(i).wait_recv()
    across(1).start()
    across(2).start()
    wu[:, 64:128, width : 2 * width] = jnp.zeros((wu.shape[0], 64, width), BF16)
    wu[:, 0:64, 2 * width : 3 * width] = jnp.zeros((wu.shape[0], 64, width), BF16)
    z_out(0)
    across(1).wait_recv()
    across(3).start()
    own_out(1)
    y_pass(0)
    loads[3].wait()
    lax.fori_loop(0, SIDE, pad_down, 0)
    z_out(1)
    across(2).wait_recv()
    own_out(2)
    y_pass(1)
    for c in loads[:3]:
        c.wait()
    up_part(0)
    z_out(2)
    across(3).wait_recv()
    own_out(3)
    y_pass(2)
    lax.fori_loop(SIDE, 2 * SIDE, pad_down, 0)
    up_part(1)
    z_out(3)
    y_pass(3)
    scaled = jnp.concatenate([jnp.where(p, weight, 0.0) for p in puts], axis=0)
    place[0] = scaled.astype(BF16)
    place[1] = (scaled - scaled.astype(BF16).astype(F32)).astype(BF16)
    up_part(2)
    up_part(3)

    def line(c, j, n):
        src, dst, to = (
            (a_up, ra_up, seg_up),
            (a_dn, ra_dn, seg_down),
            (b_up, rb_up, seg_up),
            (b_dn, rb_dn, seg_down),
        )[n]
        return pltpu.make_async_remote_copy(
            src_ref=src.at[c, j],
            dst_ref=dst.at[c, j],
            send_sem=r_s.at[c, j, n],
            recv_sem=r_r.at[c, j, n],
            device_id={"seg": to},
        )

    def down_first(c, j):
        part = mm(hp[c], wd[zpeer[j]])
        a_up[c, j] = part[0:half, 0:128].astype(BF16)
        a_dn[c, j] = part[half:chunk, 0:128].astype(BF16)
        line(c, j, 0).start()
        line(c, j, 1).start()
        b_up[c, j, half:chunk] = part[half:chunk, 384:512].astype(BF16)
        b_dn[c, j, 0:half] = part[0:half, 128:256].astype(BF16)
        keep_up[c, j] = part[0:half, 384:512]
        keep_dn[c, j] = part[half:chunk, 128:256]
        own[c, j] = part[:, 256:384]

    def down_second(c, j):
        line(c, j, 0).wait_recv()
        b_up[c, j, 0:half] = (keep_up[c, j] + ra_up[c, j].astype(F32)).astype(BF16)
        line(c, j, 2).start()
        line(c, j, 1).wait_recv()
        b_dn[c, j, half:chunk] = (keep_dn[c, j] + ra_dn[c, j].astype(F32)).astype(BF16)
        line(c, j, 3).start()

    def zsum(c, j):
        return pltpu.make_async_remote_copy(
            src_ref=zs.at[c, j],
            dst_ref=zr.at[c, j],
            send_sem=zz_s.at[c, j],
            recv_sem=zz_r.at[c, j],
            device_id={"seg": zpeer[j] * SIDE + y},
        )

    def down_third(c, j):
        line(c, j, 2).wait_recv()
        line(c, j, 3).wait_recv()
        total = own[c, j] + rb_up[c, j].astype(F32) + rb_dn[c, j].astype(F32)
        if j:
            zs[c, j] = total.astype(BF16)
            zsum(c, j).start()
        else:
            own[c, j] = total

    def home(c):
        return pltpu.make_async_remote_copy(
            src_ref=fb.at[c],
            dst_ref=rb1.at[c],
            send_sem=th_s.at[c],
            recv_sem=th_r.at[c],
            device_id=at_zh(OFF[c]),
        )

    def finish(c):
        total = own[c, 0]
        for j in range(1, SIDE):
            zsum(c, j).wait_recv()
            total += zr[c, j].astype(F32)
        if c:
            fb[c] = total.astype(BF16)
            home(c).start()
        else:
            rb1[c] = total.astype(BF16)

    def share(c, i):
        to = (x + i) % xs
        return pltpu.make_async_remote_copy(
            src_ref=rb1.at[c, pl.ds(to * PACK, PACK)],
            dst_ref=rb2.at[c, pl.ds(x * PACK, PACK)],
            send_sem=tx_s.at[c, i],
            recv_sem=tx_r.at[c, i],
            device_id=at_x(i),
        )

    def spread(c):
        if c:
            home(c).wait_recv()
        for i in range(1, xs):
            share(c, i).start()
        rb2[c, mine, :] = rb1[c, mine, :]

    order = [(c, j) for c in (3, 1, 2, 0) for j in (1, 2, 3, 0)]
    done = {3: 0, 1: 0, 2: 0, 0: 0}
    for n in range(len(order) + LAG3 + LAG4):
        if n < len(order):
            down_first(*order[n])
        if 0 <= n - LAG2 < len(order):
            down_second(*order[n - LAG2])
        if 0 <= n - LAG3 < len(order):
            down_third(*order[n - LAG3])
        m = n - LAG3 - LAG4
        if 0 <= m < len(order) and m % SIDE == SIDE - 1 and order[m][0]:
            finish(order[m][0])
    spread(3)
    spread(1)
    finish(0)
    spread(0)
    spread(2)

    for i in range(1, xs):
        first_x(i).wait_send()
        other_x(i).wait_send()
    for c in range(SIDE):
        if c:
            across(c).wait_send()
            home(c).wait_send()
        for i in range(1, xs):
            share(c, i).wait_send()
        for j in range(SIDE):
            if j:
                zcopy(c, j).wait_send()
                zsum(c, j).wait_send()
            for n in range(4):
                ycopy(c, j, n).wait_send()
                line(c, j, n).wait_send()
    for c in range(SIDE):
        for i in range(1, xs):
            share(c, i).wait_recv()
    got = rb2[...].reshape(rows, LANES)
    mixed = mm(place[0], got) + mm(place[1], got)
    out_ref[:, 0:128] = mixed[0:tokens].astype(BF16)
    tail = mixed[tokens : 2 * tokens, 0:64] + mixed[2 * tokens : 3 * tokens, 64:128]
    out_ref[:, 128:192] = tail.astype(BF16)


def shards(experts, tokens, expert_ids, route_weight, w_up, w_down):
    segs = SIDE * SIDE
    xs = experts // SIDE
    chunk = xs * PACK
    half = chunk // 2
    width = w_up.shape[2]
    count, block = tokens.shape
    vm = pltpu.VMEM
    dma = pltpu.SemaphoreType.DMA
    each = (SIDE, SIDE)
    return pl.pallas_call(
        functools.partial(layer, experts),
        out_shape=jax.ShapeDtypeStruct(tokens.shape, BF16),
        in_specs=[pl.BlockSpec(memory_space=vm)] * 3 + [pl.BlockSpec(memory_space=pl.ANY)] * 2,
        out_specs=pl.BlockSpec(memory_space=vm),
        scratch_shapes=[
            vm((SIDE, chunk, LANES), BF16),
            vm((SIDE - 1, chunk, LANES), BF16),
            vm((SIDE, segs, chunk, LANES), BF16),
            vm((segs, LANES, 3 * width), BF16),
            vm((width, segs * block), BF16),
            vm((SIDE, 3 * width, SIDE * LANES), BF16),
            vm((SIDE, chunk, 3 * width), BF16),
            vm((2, 3 * count, SIDE * chunk), BF16),
            vm((*each, half, LANES), BF16),
            vm((*each, half, LANES), BF16),
            vm((*each, chunk, LANES), BF16),
            vm((*each, chunk, LANES), BF16),
            vm((*each, half, LANES), BF16),
            vm((*each, half, LANES), BF16),
            vm((*each, chunk, LANES), BF16),
            vm((*each, chunk, LANES), BF16),
            vm((*each, half, LANES), F32),
            vm((*each, half, LANES), F32),
            vm((*each, chunk, LANES), F32),
            vm((*each, chunk, LANES), BF16),
            vm((*each, chunk, LANES), BF16),
            vm((SIDE, chunk, LANES), BF16),
            vm((SIDE, chunk, LANES), BF16),
            vm((SIDE, chunk, LANES), BF16),
            dma((4,)),
            dma((2, xs)),
            dma((2, xs)),
            dma((SIDE,)),
            dma((SIDE,)),
            dma(each),
            dma(each),
            dma((*each, 4)),
            dma((*each, 4)),
            dma((*each, 4)),
            dma((*each, 4)),
            dma(each),
            dma(each),
            dma((SIDE,)),
            dma((SIDE,)),
            dma((SIDE, xs)),
            dma((SIDE, xs)),
        ],
        compiler_params=pltpu.CompilerParams(
            collective_id=0, has_side_effects=True, vmem_limit_bytes=56 * 2**20
        ),
    )(
        tokens,
        expert_ids.T,
        route_weight.T,
        w_up.reshape(segs, block, width),
        w_down.reshape(width, segs * block),
    )


def solution(mesh):
    placed = (
        P(("dp", "expert"), "seg"),
        P(("dp", "expert"), None),
        P(("dp", "expert"), None),
        P("expert", None, "seg"),
        P("expert", "seg", None),
    )
    return jax.shard_map(
        functools.partial(shards, mesh.shape["expert"]),
        mesh=mesh,
        in_specs=placed,
        out_specs=P(("dp", "expert"), "seg"),
        check_vma=False,
    )
```

```python
import functools

import jax
import jax.numpy as jnp
from jax import lax
from jax.experimental import pallas as pl
from jax.experimental.pallas import tpu as pltpu
from jax.sharding import PartitionSpec as P

CAP = 21
PACK = 32
LANES = 128
SIDE = 4
OFF = (0, 1, 3, 2)
GATHER_DIRECT = (0, 0, 0, 0)
SUM_DIRECT = (0, 0, 0, 0)
ORDER = (
    0, 132, 136, 32, 17, 4, 8, 18, 140, 19, 33, 36, 21, 40, 34, 12,
    35, 22, 23, 25, 37, 26, 44, 27, 48, 29, 38, 39, 30, 41, 31, 42,
    43, 45, 52, 46, 69, 70, 47, 71, 56, 68, 85, 86, 60, 87, 77, 78,
    84, 79, 76, 101, 73, 74, 102, 75, 72, 65, 103, 93, 66, 94, 67, 100,
    64, 95, 92, 89, 90, 91, 88, 81, 109, 82, 116, 110, 83, 80, 111, 108,
    105, 106, 107, 104, 97, 124, 98, 99, 96, 120, 112,
)
F32 = jnp.float32
BF16 = jnp.bfloat16


def mm(a, b):
    return jnp.dot(a, b, preferred_element_type=F32)


def mm_t(a, b):
    return lax.dot_general(a, b, (((0,), (0,)), ((), ())), preferred_element_type=F32)


def layer(
    experts, tok_ref, ids_ref, rw_ref, wup_ref, wdn_ref, out_ref,
    sbuf, mid, ag, wu, wraw, wd, hp, place, a_up, a_dn, b_up, b_dn, b_far, ra_up, ra_dn, rb_up, rb_dn, rb_far,
    keep_up, keep_dn, own, zs, zr, fb, rb2,
    wsem, hint, dx_s, dx_r, dz_s, dz_r, z_s, z_r, y_s, y_r, r_s, r_r, zz_s, zz_r, th_s, th_r,
):
    topk = ids_ref.shape[0]
    tokens = tok_ref.shape[0]
    xs = experts // SIDE
    chunk = xs * PACK
    half = chunk // 2
    rows = SIDE * chunk
    width = wup_ref.shape[2]
    e = lax.axis_index("expert")
    s = lax.axis_index("seg")
    zh, x = e // xs, e % xs
    zl, y = s // SIDE, s % SIDE
    up = (y + 1) % SIDE
    down = (y + SIDE - 1) % SIDE
    far = (y + 2) % SIDE
    zpeer = [zl, zl + 1 - 2 * (zl % 2), (zl + 2) % SIDE, SIDE - 1 - zl]
    seg_up, seg_down, seg_far = zl * SIDE + up, zl * SIDE + down, zl * SIDE + far

    def at_zh(off):
        return {"expert": (zh + SIDE + off) % SIDE * xs + x}

    def at_x(i):
        return {"expert": zh * xs + (x + i) % xs}

    barrier = pltpu.get_barrier_semaphore()
    near = [at_x(i) for i in range(1, xs)] + [at_zh(1), at_zh(-1)]
    near += [{"seg": seg_up}, {"seg": seg_down}, {"seg": seg_far}]
    near += [{"seg": zpeer[j] * SIDE + y} for j in range(1, SIDE)]
    for to in near:
        pl.semaphore_signal(barrier, inc=1, device_id=to)

    loads = [
        pltpu.make_async_copy(wup_ref.at[:, 0:128, :], wu.at[:, :, 0:width], wsem.at[0]),
        pltpu.make_async_copy(wup_ref.at[:, 128:192, :], wu.at[:, 0:64, width : 2 * width], wsem.at[1]),
        pltpu.make_async_copy(wup_ref.at[:, 128:192, :], wu.at[:, 64:128, 2 * width : 3 * width], wsem.at[2]),
        pltpu.make_async_copy(wdn_ref, wraw, wsem.at[3]),
    ]
    for c in loads:
        c.start()

    table = jnp.concatenate([ids_ref[...].astype(F32), rw_ref[...]], axis=0).T
    ids, rw = table[:, 0:topk], table[:, topk : 2 * topk]
    norm = rw / jnp.sum(rw, axis=1, keepdims=True)
    lane = lax.broadcasted_iota(jnp.int32, (tokens, rows), 1)
    lane_c, lane_x, lane_r = lane // chunk, lane % chunk // PACK, lane % PACK
    lane_off = jnp.where(lane_c == 0, 0, jnp.where(lane_c == 1, 1, 5 - lane_c))
    lane_e = ((zh + SIDE - lane_off) % SIDE * xs + lane_x).astype(F32)
    weight = jnp.zeros((tokens, rows), F32)
    named = jnp.zeros((tokens, rows), F32)
    for k in range(topk):
        hit = ids[:, k : k + 1] == lane_e
        named = jnp.where(hit, 1.0, named)
        weight = jnp.where(hit, norm[:, k : k + 1], weight)
    earlier = lax.broadcasted_iota(jnp.int32, (tokens, tokens), 1) < lax.broadcasted_iota(
        jnp.int32, (tokens, tokens), 0
    )
    slot = mm(jnp.where(earlier, 1.0, 0.0).astype(BF16), named.astype(BF16)).astype(jnp.int32)
    main = lane_r < CAP
    puts = (main & (slot == lane_r), ~main & (slot == lane_r - CAP), ~main & (slot == lane_r - 10))
    tok = tok_ref[...]
    rest = tok[:, 128:192].astype(F32)
    blank = jnp.zeros((tokens, 64), F32)
    source = jnp.concatenate(
        [
            tok[:, 0:128],
            jnp.concatenate([rest, blank], axis=1).astype(BF16),
            jnp.concatenate([blank, rest], axis=1).astype(BF16),
        ],
        axis=0,
    )
    onehot = jnp.concatenate([jnp.where(p, named, 0.0) for p in puts], axis=0)
    sbuf[...] = mm_t(onehot.astype(BF16), source).astype(BF16).reshape(SIDE, chunk, LANES)

    pl.semaphore_wait(barrier, len(near))

    def across(c):
        return pltpu.make_async_remote_copy(
            src_ref=sbuf.at[c],
            dst_ref=mid.at[c],
            send_sem=dz_s.at[c],
            recv_sem=dz_r.at[c],
            device_id=at_zh(-OFF[c]),
        )

    def over_x(c, i):
        to = (x + i) % xs
        return pltpu.make_async_remote_copy(
            src_ref=(mid if c else sbuf).at[c, pl.ds(to * PACK, PACK)],
            dst_ref=ag.at[c, s, pl.ds(x * PACK, PACK)],
            send_sem=dx_s.at[c, i],
            recv_sem=dx_r.at[c, i],
            device_id=at_x(i),
        )

    mine = pl.ds(x * PACK, PACK)

    def to_x(c):
        if c:
            across(c).wait_recv()
        for i in range(1, xs):
            over_x(c, i).start()
        ag[c, s, mine, :] = (mid if c else sbuf)[c, mine, :]

    def zcopy(c, j):
        return pltpu.make_async_remote_copy(
            src_ref=ag.at[c, s],
            dst_ref=ag.at[c, s],
            send_sem=z_s.at[c, j],
            recv_sem=z_r.at[c, j],
            device_id={"seg": zpeer[j] * SIDE + y},
        )

    def z_arrival(c, j):
        g = zpeer[j] * SIDE + y
        return pltpu.make_async_remote_copy(
            src_ref=ag.at[c, g],
            dst_ref=ag.at[c, g],
            send_sem=z_s.at[c, j],
            recv_sem=z_r.at[c, j],
            device_id={"seg": g},
        )

    def ycopy(c, j, line):
        col, part, to = (
            (y, pl.ds(0, chunk), seg_up),
            (y, pl.ds(0, chunk), seg_down),
            (down, pl.ds(0, half), seg_up),
            (up, pl.ds(half, half), seg_down),
            (y, pl.ds(0, chunk), seg_far),
        )[line]
        g = zpeer[j] * SIDE + col
        return pltpu.make_async_remote_copy(
            src_ref=ag.at[c, g, part],
            dst_ref=ag.at[c, g, part],
            send_sem=y_s.at[c, j, line],
            recv_sem=y_r.at[c, j, line],
            device_id={"seg": to},
        )

    def y_arrival(c, j, line):
        col, part = (
            (down, pl.ds(0, chunk)),
            (up, pl.ds(0, chunk)),
            (far, pl.ds(0, half)),
            (far, pl.ds(half, half)),
            (far, pl.ds(0, chunk)),
        )[line]
        g = zpeer[j] * SIDE + col
        return pltpu.make_async_remote_copy(
            src_ref=ag.at[c, g, part],
            dst_ref=ag.at[c, g, part],
            send_sem=y_s.at[c, j, line],
            recv_sem=y_r.at[c, j, line],
            device_id={"seg": seg_up},
        )

    def y_send(c, j):
        ycopy(c, j, 0).start()
        ycopy(c, j, 1).start()
        if GATHER_DIRECT[c]:
            ycopy(c, j, 4).start()

    def own_out(c):
        for j in range(1, SIDE):
            zcopy(c, j).start()
        y_send(c, 0)

    def z_out(c, j):
        z_arrival(c, j).wait_recv()
        y_send(c, j)

    def y_pass(c, j):
        y_arrival(c, j, 0).wait_recv()
        ycopy(c, j, 2).start()
        y_arrival(c, j, 1).wait_recv()
        ycopy(c, j, 3).start()

    r = lax.broadcasted_iota(jnp.int32, (chunk, width), 0) % PACK

    def up_part(c):
        for j in range(SIDE):
            for n in (0, 1, 4) if GATHER_DIRECT[c] else (2, 3):
                y_arrival(c, j, n).wait_recv()
        lhs = jnp.concatenate([ag[c, g] for g in range(SIDE * SIDE)], axis=1)
        u = mm(lhs, wu[...].reshape(SIDE * SIDE * LANES, 3 * width))
        v = u[:, 0:width] + jnp.where(
            r < 11,
            pltpu.roll(u[:, width : 2 * width], chunk - 21, 0),
            pltpu.roll(u[:, 2 * width : 3 * width], chunk - 10, 0),
        )
        h = jnp.where(r < CAP, v / (1.0 + jnp.exp(-v)), 0.0)
        hp[c, :, 0:width] = h.astype(BF16)
        hp[c, :, width : 2 * width] = jnp.where(r < CAP, 0.0, pltpu.roll(h, 21, 0)).astype(BF16)
        hp[c, :, 2 * width : 3 * width] = jnp.where(r < CAP, 0.0, pltpu.roll(h, 10, 0)).astype(BF16)

    left = lax.broadcasted_iota(jnp.int32, (width, LANES), 1) < 64

    def pad_down(i, c):
        z, q = i // 2, i % 2
        base = pl.multiple_of(i * 384, 128)
        a = wraw[:, pl.ds(base, 128)]
        b = wraw[:, pl.ds(base + 128, 128)].astype(F32)
        g = wraw[:, pl.ds(base + 256, 128)].astype(F32)
        b_turn, g_turn = pltpu.roll(b, 64, 1), pltpu.roll(g, 64, 1)
        to0 = pl.multiple_of((2 * q + 6 - y) % SIDE * LANES, LANES)
        to1 = pl.multiple_of((2 * q + 7 - y) % SIDE * LANES, LANES)
        wd[z, 0:width, pl.ds(to0, LANES)] = a
        wd[z, width : 2 * width, pl.ds(to0, LANES)] = jnp.where(left, b, 0.0).astype(BF16)
        wd[z, 2 * width : 3 * width, pl.ds(to0, LANES)] = jnp.where(left, 0.0, b_turn).astype(BF16)
        wd[z, 0:width, pl.ds(to1, LANES)] = jnp.where(left, b_turn, g_turn).astype(BF16)
        wd[z, width : 2 * width, pl.ds(to1, LANES)] = jnp.where(left, g_turn, 0.0).astype(BF16)
        wd[z, 2 * width : 3 * width, pl.ds(to1, LANES)] = jnp.where(left, 0.0, g).astype(BF16)
        return c

    pl.semaphore_signal(hint, inc=1, device_id=at_zh(-1))
    across(1).start()
    across(2).start()
    to_x(0)
    loads[3].wait()
    lax.fori_loop(0, SIDE, pad_down, 0)
    pl.semaphore_wait(hint, 1)
    across(3).start()
    lax.fori_loop(SIDE, 2 * SIDE, pad_down, 0)

    def arrived(c):
        for i in range(1, xs):
            over_x(c, i).wait_recv()
        own_out(c)
        if c == 0:
            wu[:, 64:128, width : 2 * width] = jnp.zeros((wu.shape[0], 64, width), BF16)
            wu[:, 0:64, 2 * width : 3 * width] = jnp.zeros((wu.shape[0], 64, width), BF16)
            for load in loads[:3]:
                load.wait()
            scaled = jnp.concatenate([jnp.where(p, weight, 0.0) for p in puts], axis=0)
            place[0] = scaled.astype(BF16)
            place[1] = (scaled - scaled.astype(BF16).astype(F32)).astype(BF16)

    def line(c, j, n):
        src, dst, to = (
            (a_up, ra_up, seg_up),
            (a_dn, ra_dn, seg_down),
            (b_up, rb_up, seg_up),
            (b_dn, rb_dn, seg_down),
            (b_far, rb_far, seg_far),
        )[n]
        return pltpu.make_async_remote_copy(
            src_ref=src.at[c, j],
            dst_ref=dst.at[c, j],
            send_sem=r_s.at[c, j, n],
            recv_sem=r_r.at[c, j, n],
            device_id={"seg": to},
        )

    def down_first(c, j):
        part = mm(hp[c], wd[zpeer[j]])
        own[c, j] = part[:, 256:384]
        if SUM_DIRECT[c]:
            b_far[c, j] = part[:, 0:128].astype(BF16)
            line(c, j, 4).start()
            b_up[c, j] = part[:, 384:512].astype(BF16)
            line(c, j, 2).start()
            b_dn[c, j] = part[:, 128:256].astype(BF16)
            line(c, j, 3).start()
            return
        a_up[c, j] = part[0:half, 0:128].astype(BF16)
        a_dn[c, j] = part[half:chunk, 0:128].astype(BF16)
        line(c, j, 0).start()
        line(c, j, 1).start()
        b_up[c, j, half:chunk] = part[half:chunk, 384:512].astype(BF16)
        b_dn[c, j, 0:half] = part[0:half, 128:256].astype(BF16)
        keep_up[c, j] = part[0:half, 384:512]
        keep_dn[c, j] = part[half:chunk, 128:256]

    def down_second(c, j):
        line(c, j, 0).wait_recv()
        b_up[c, j, 0:half] = (keep_up[c, j] + ra_up[c, j].astype(F32)).astype(BF16)
        line(c, j, 2).start()
        line(c, j, 1).wait_recv()
        b_dn[c, j, half:chunk] = (keep_dn[c, j] + ra_dn[c, j].astype(F32)).astype(BF16)
        line(c, j, 3).start()

    def zsum(c, j):
        return pltpu.make_async_remote_copy(
            src_ref=zs.at[c, j],
            dst_ref=zr.at[c, j],
            send_sem=zz_s.at[c, j],
            recv_sem=zz_r.at[c, j],
            device_id={"seg": zpeer[j] * SIDE + y},
        )

    def down_third(c, j):
        line(c, j, 2).wait_recv()
        line(c, j, 3).wait_recv()
        total = own[c, j] + rb_up[c, j].astype(F32) + rb_dn[c, j].astype(F32)
        if SUM_DIRECT[c]:
            line(c, j, 4).wait_recv()
            total += rb_far[c, j].astype(F32)
        if j:
            zs[c, j] = total.astype(BF16)
            zsum(c, j).start()
        else:
            own[c, j] = total

    def home(c, i):
        to = (x + i) % xs
        return pltpu.make_async_remote_copy(
            src_ref=fb.at[c, pl.ds(to * PACK, PACK)],
            dst_ref=rb2.at[c, pl.ds(x * PACK, PACK)],
            send_sem=th_s.at[c, i],
            recv_sem=th_r.at[c, i],
            device_id={"expert": (zh + OFF[c]) % SIDE * xs + to},
        )

    def finish(c):
        total = own[c, 0]
        for j in range(1, SIDE):
            zsum(c, j).wait_recv()
            total += zr[c, j].astype(F32)
        fb[c] = total.astype(BF16)
        for i in range(c == 0, xs):
            home(c, i).start()
        if c == 0:
            rb2[0, mine, :] = fb[0, mine, :]

    steps = (
        lambda c, j: arrived(c),
        z_out,
        y_pass,
        lambda c, j: up_part(c),
        down_first,
        down_second,
        down_third,
        lambda c, j: finish(c),
        lambda c, j: to_x(c),
    )
    for step in ORDER:
        steps[step // 16](step % 16 // 4, step % 4)

    for c in range(SIDE):
        if c:
            across(c).wait_send()
        for i in range(1, xs):
            over_x(c, i).wait_send()
        for i in range(c == 0, xs):
            home(c, i).wait_send()
        for j in range(SIDE):
            if j:
                zcopy(c, j).wait_send()
                zsum(c, j).wait_send()
            for n in (0, 1, 4) if GATHER_DIRECT[c] else range(4):
                ycopy(c, j, n).wait_send()
            for n in (2, 3, 4) if SUM_DIRECT[c] else range(4):
                line(c, j, n).wait_send()
    for c in range(SIDE):
        for i in range(c == 0, xs):
            home(c, i).wait_recv()
    got = rb2[...].reshape(rows, LANES)
    mixed = mm(place[0], got) + mm(place[1], got)
    out_ref[:, 0:128] = mixed[0:tokens].astype(BF16)
    tail = mixed[tokens : 2 * tokens, 0:64] + mixed[2 * tokens : 3 * tokens, 64:128]
    out_ref[:, 128:192] = tail.astype(BF16)


def shards(experts, tokens, expert_ids, route_weight, w_up, w_down):
    segs = SIDE * SIDE
    xs = experts // SIDE
    chunk = xs * PACK
    half = chunk // 2
    width = w_up.shape[2]
    count, block = tokens.shape
    vm = pltpu.VMEM
    dma = pltpu.SemaphoreType.DMA
    each = (SIDE, SIDE)
    return pl.pallas_call(
        functools.partial(layer, experts),
        out_shape=jax.ShapeDtypeStruct(tokens.shape, BF16),
        in_specs=[pl.BlockSpec(memory_space=vm)] * 3 + [pl.BlockSpec(memory_space=pl.ANY)] * 2,
        out_specs=pl.BlockSpec(memory_space=vm),
        scratch_shapes=[
            vm((SIDE, chunk, LANES), BF16),
            vm((SIDE, chunk, LANES), BF16),
            vm((SIDE, segs, chunk, LANES), BF16),
            vm((segs, LANES, 3 * width), BF16),
            vm((width, segs * block), BF16),
            vm((SIDE, 3 * width, SIDE * LANES), BF16),
            vm((SIDE, chunk, 3 * width), BF16),
            vm((2, 3 * count, SIDE * chunk), BF16),
            vm((*each, half, LANES), BF16),
            vm((*each, half, LANES), BF16),
            vm((*each, chunk, LANES), BF16),
            vm((*each, chunk, LANES), BF16),
            vm((*each, chunk, LANES), BF16),
            vm((*each, half, LANES), BF16),
            vm((*each, half, LANES), BF16),
            vm((*each, chunk, LANES), BF16),
            vm((*each, chunk, LANES), BF16),
            vm((*each, chunk, LANES), BF16),
            vm((*each, half, LANES), F32),
            vm((*each, half, LANES), F32),
            vm((*each, chunk, LANES), F32),
            vm((*each, chunk, LANES), BF16),
            vm((*each, chunk, LANES), BF16),
            vm((SIDE, chunk, LANES), BF16),
            vm((SIDE, chunk, LANES), BF16),
            dma((4,)),
            pltpu.SemaphoreType.REGULAR,
            dma((SIDE, xs)),
            dma((SIDE, xs)),
            dma((SIDE,)),
            dma((SIDE,)),
            dma(each),
            dma(each),
            dma((*each, 5)),
            dma((*each, 5)),
            dma((*each, 5)),
            dma((*each, 5)),
            dma(each),
            dma(each),
            dma((SIDE, xs)),
            dma((SIDE, xs)),
        ],
        compiler_params=pltpu.CompilerParams(
            collective_id=0, has_side_effects=True, vmem_limit_bytes=56 * 2**20
        ),
    )(
        tokens,
        expert_ids.T,
        route_weight.T,
        w_up.reshape(segs, block, width),
        w_down.reshape(width, segs * block),
    )


def solution(mesh):
    placed = (
        P(("dp", "expert"), "seg"),
        P(("dp", "expert"), None),
        P(("dp", "expert"), None),
        P("expert", None, "seg"),
        P("expert", "seg", None),
    )
    return jax.shard_map(
        functools.partial(shards, mesh.shape["expert"]),
        mesh=mesh,
        in_specs=placed,
        out_specs=P(("dp", "expert"), "seg"),
        check_vma=False,
    )
```

```python
import functools

import jax
import jax.numpy as jnp
from jax import lax
from jax.experimental import pallas as pl
from jax.experimental.pallas import tpu as pltpu
from jax.sharding import PartitionSpec as P

CAP = 21
PACK = 32
LANES = 128
SIDE = 4
OFF = (0, 1, 3, 2)
GATHER_DIRECT = (1, 0, 0, 0)
SUM_DIRECT = (0, 0, 0, 1)
ORDER = (
    0, 132, 136, 17, 48, 4, 8, 18, 19, 140, 49, 36, 21, 40, 22, 50,
    23, 12, 25, 52, 51, 37, 26, 56, 38, 27, 39, 44, 29, 41, 53, 30,
    42, 54, 31, 43, 55, 69, 70, 45, 71, 68, 46, 60, 57, 58, 47, 59,
    85, 73, 86, 74, 87, 75, 84, 72, 61, 62, 63, 77, 101, 89, 78, 79,
    102, 90, 76, 65, 103, 91, 66, 67, 100, 88, 64, 109, 105, 110, 116, 111,
    106, 108, 81, 107, 82, 83, 104, 124, 80, 97, 98, 99, 120, 96,
)
F32 = jnp.float32
BF16 = jnp.bfloat16


def mm(a, b):
    return jnp.dot(a, b, preferred_element_type=F32)


def mm_t(a, b):
    return lax.dot_general(a, b, (((0,), (0,)), ((), ())), preferred_element_type=F32)


def layer(
    experts, tok_hbm, ids_hbm, rw_hbm, wup_ref, wdn_ref, out_ref,
    tok_ref, ids_ref, rw_ref, sbuf, mid, ag, wu, wraw, wd, acc, hp, place, a_up, a_dn, b_up, b_dn, b_far, ra_up, ra_dn, rb_up, rb_dn, rb_far,
    keep_up, keep_dn, own, zs, zr, fb, rb0, rb2,
    isem, wsem, hint, dx_s, dx_r, dz_s, dz_r, z_s, z_r, y_s, y_r, r_s, r_r, zz_s, zz_r, th_s, th_r, t0_s, t0_r,
):
    topk = ids_ref.shape[0]
    tokens = tok_ref.shape[0]
    xs = experts // SIDE
    chunk = xs * PACK
    half = chunk // 2
    rows = SIDE * chunk
    width = wup_ref.shape[2]
    e = lax.axis_index("expert")
    s = lax.axis_index("seg")
    zh, x = e // xs, e % xs
    zl, y = s // SIDE, s % SIDE
    up = (y + 1) % SIDE
    down = (y + SIDE - 1) % SIDE
    far = (y + 2) % SIDE
    zpeer = [zl, zl + 1 - 2 * (zl % 2), (zl + 2) % SIDE, SIDE - 1 - zl]
    seg_up, seg_down, seg_far = zl * SIDE + up, zl * SIDE + down, zl * SIDE + far

    def at_zh(off):
        return {"expert": (zh + SIDE + off) % SIDE * xs + x}

    def at_x(i):
        return {"expert": zh * xs + (x + i) % xs}

    small = [
        pltpu.make_async_copy(tok_hbm, tok_ref, isem.at[0]),
        pltpu.make_async_copy(ids_hbm, ids_ref, isem.at[1]),
        pltpu.make_async_copy(rw_hbm, rw_ref, isem.at[2]),
    ]
    for c in small:
        c.start()
    barrier = pltpu.get_barrier_semaphore()
    near = [at_x(i) for i in range(1, xs)] + [at_zh(1), at_zh(-1)]
    near += [{"seg": seg_up}, {"seg": seg_down}, {"seg": seg_far}]
    near += [{"seg": zpeer[j] * SIDE + y} for j in range(1, SIDE)]
    for to in near:
        pl.semaphore_signal(barrier, inc=1, device_id=to)

    loads = [
        pltpu.make_async_copy(wup_ref.at[:, 0:128, :], wu.at[:, :, 0:width], wsem.at[0]),
        pltpu.make_async_copy(wup_ref.at[:, 128:192, :], wu.at[:, 0:64, width : 2 * width], wsem.at[1]),
        pltpu.make_async_copy(wup_ref.at[:, 128:192, :], wu.at[:, 64:128, 2 * width : 3 * width], wsem.at[2]),
        pltpu.make_async_copy(wdn_ref, wraw, wsem.at[3]),
    ]
    for c in loads:
        c.start()

    for c in small:
        c.wait()
    table = jnp.concatenate([ids_ref[...].astype(F32), rw_ref[...]], axis=0).T
    ids, rw = table[:, 0:topk], table[:, topk : 2 * topk]
    norm = rw / jnp.sum(rw, axis=1, keepdims=True)
    lane = lax.broadcasted_iota(jnp.int32, (tokens, rows), 1)
    lane_c, lane_x, lane_r = lane // chunk, lane % chunk // PACK, lane % PACK
    lane_off = jnp.where(lane_c == 0, 0, jnp.where(lane_c == 1, 1, 5 - lane_c))
    lane_e = ((zh + SIDE - lane_off) % SIDE * xs + lane_x).astype(F32)
    weight = jnp.zeros((tokens, rows), F32)
    named = jnp.zeros((tokens, rows), F32)
    for k in range(topk):
        hit = ids[:, k : k + 1] == lane_e
        named = jnp.where(hit, 1.0, named)
        weight = jnp.where(hit, norm[:, k : k + 1], weight)
    earlier = lax.broadcasted_iota(jnp.int32, (tokens, tokens), 1) < lax.broadcasted_iota(
        jnp.int32, (tokens, tokens), 0
    )
    slot = mm(jnp.where(earlier, 1.0, 0.0).astype(BF16), named.astype(BF16)).astype(jnp.int32)
    main = lane_r < CAP
    puts = (main & (slot == lane_r), ~main & (slot == lane_r - CAP), ~main & (slot == lane_r - 10))
    tok = tok_ref[...]
    rest = tok[:, 128:192].astype(F32)
    blank = jnp.zeros((tokens, 64), F32)
    source = jnp.concatenate(
        [
            tok[:, 0:128],
            jnp.concatenate([rest, blank], axis=1).astype(BF16),
            jnp.concatenate([blank, rest], axis=1).astype(BF16),
        ],
        axis=0,
    )
    onehot = jnp.concatenate([jnp.where(p, named, 0.0) for p in puts], axis=0)
    sbuf[...] = mm_t(onehot.astype(BF16), source).astype(BF16).reshape(SIDE, chunk, LANES)

    pl.semaphore_wait(barrier, len(near))

    def across(c):
        return pltpu.make_async_remote_copy(
            src_ref=sbuf.at[c],
            dst_ref=mid.at[c],
            send_sem=dz_s.at[c],
            recv_sem=dz_r.at[c],
            device_id=at_zh(-OFF[c]),
        )

    def over_x(c, i):
        to = (x + i) % xs
        return pltpu.make_async_remote_copy(
            src_ref=(mid if c else sbuf).at[c, pl.ds(to * PACK, PACK)],
            dst_ref=ag.at[c, s, pl.ds(x * PACK, PACK)],
            send_sem=dx_s.at[c, i],
            recv_sem=dx_r.at[c, i],
            device_id=at_x(i),
        )

    mine = pl.ds(x * PACK, PACK)

    def to_x(c):
        if c:
            across(c).wait_recv()
        for i in range(1, xs):
            over_x(c, i).start()
        ag[c, s, mine, :] = (mid if c else sbuf)[c, mine, :]

    def zcopy(c, j):
        return pltpu.make_async_remote_copy(
            src_ref=ag.at[c, s],
            dst_ref=ag.at[c, s],
            send_sem=z_s.at[c, j],
            recv_sem=z_r.at[c, j],
            device_id={"seg": zpeer[j] * SIDE + y},
        )

    def z_arrival(c, j):
        g = zpeer[j] * SIDE + y
        return pltpu.make_async_remote_copy(
            src_ref=ag.at[c, g],
            dst_ref=ag.at[c, g],
            send_sem=z_s.at[c, j],
            recv_sem=z_r.at[c, j],
            device_id={"seg": g},
        )

    def ycopy(c, j, line):
        col, part, to = (
            (y, pl.ds(0, chunk), seg_up),
            (y, pl.ds(0, chunk), seg_down),
            (down, pl.ds(0, half), seg_up),
            (up, pl.ds(half, half), seg_down),
            (y, pl.ds(0, chunk), seg_far),
        )[line]
        g = zpeer[j] * SIDE + col
        return pltpu.make_async_remote_copy(
            src_ref=ag.at[c, g, part],
            dst_ref=ag.at[c, g, part],
            send_sem=y_s.at[c, j, line],
            recv_sem=y_r.at[c, j, line],
            device_id={"seg": to},
        )

    def y_arrival(c, j, line):
        col, part = (
            (down, pl.ds(0, chunk)),
            (up, pl.ds(0, chunk)),
            (far, pl.ds(0, half)),
            (far, pl.ds(half, half)),
            (far, pl.ds(0, chunk)),
        )[line]
        g = zpeer[j] * SIDE + col
        return pltpu.make_async_remote_copy(
            src_ref=ag.at[c, g, part],
            dst_ref=ag.at[c, g, part],
            send_sem=y_s.at[c, j, line],
            recv_sem=y_r.at[c, j, line],
            device_id={"seg": seg_up},
        )

    def y_send(c, j):
        ycopy(c, j, 0).start()
        ycopy(c, j, 1).start()
        if GATHER_DIRECT[c]:
            ycopy(c, j, 4).start()

    def own_out(c):
        for j in range(1, SIDE):
            zcopy(c, j).start()
        y_send(c, 0)

    def z_out(c, j):
        z_arrival(c, j).wait_recv()
        y_send(c, j)

    def y_pass(c, j):
        y_arrival(c, j, 0).wait_recv()
        ycopy(c, j, 2).start()
        y_arrival(c, j, 1).wait_recv()
        ycopy(c, j, 3).start()

    r = lax.broadcasted_iota(jnp.int32, (chunk, width), 0) % PACK

    summed = [0] * SIDE

    def up_part(c, j):
        for n in (0, 1, 4) if GATHER_DIRECT[c] else (2, 3):
            y_arrival(c, j, n).wait_recv()
        g = zpeer[j] * SIDE
        lhs = jnp.concatenate([ag[c, g + i] for i in range(SIDE)], axis=1)
        u = mm(lhs, wu[pl.ds(g, SIDE)].reshape(SIDE * LANES, 3 * width))
        if summed[c]:
            u += acc[c]
        summed[c] += 1
        if summed[c] < SIDE:
            acc[c] = u
            return
        v = u[:, 0:width] + jnp.where(
            r < 11,
            pltpu.roll(u[:, width : 2 * width], chunk - 21, 0),
            pltpu.roll(u[:, 2 * width : 3 * width], chunk - 10, 0),
        )
        h = jnp.where(r < CAP, v / (1.0 + jnp.exp(-v)), 0.0)
        hp[c, :, 0:width] = h.astype(BF16)
        hp[c, :, width : 2 * width] = jnp.where(r < CAP, 0.0, pltpu.roll(h, 21, 0)).astype(BF16)
        hp[c, :, 2 * width : 3 * width] = jnp.where(r < CAP, 0.0, pltpu.roll(h, 10, 0)).astype(BF16)

    left = lax.broadcasted_iota(jnp.int32, (width, LANES), 1) < 64

    def pad_down(i, c):
        z, q = i // 2, i % 2
        base = pl.multiple_of(i * 384, 128)
        a = wraw[:, pl.ds(base, 128)]
        b = wraw[:, pl.ds(base + 128, 128)].astype(F32)
        g = wraw[:, pl.ds(base + 256, 128)].astype(F32)
        b_turn, g_turn = pltpu.roll(b, 64, 1), pltpu.roll(g, 64, 1)
        to0 = pl.multiple_of((2 * q + 6 - y) % SIDE * LANES, LANES)
        to1 = pl.multiple_of((2 * q + 7 - y) % SIDE * LANES, LANES)
        wd[z, 0:width, pl.ds(to0, LANES)] = a
        wd[z, width : 2 * width, pl.ds(to0, LANES)] = jnp.where(left, b, 0.0).astype(BF16)
        wd[z, 2 * width : 3 * width, pl.ds(to0, LANES)] = jnp.where(left, 0.0, b_turn).astype(BF16)
        wd[z, 0:width, pl.ds(to1, LANES)] = jnp.where(left, b_turn, g_turn).astype(BF16)
        wd[z, width : 2 * width, pl.ds(to1, LANES)] = jnp.where(left, g_turn, 0.0).astype(BF16)
        wd[z, 2 * width : 3 * width, pl.ds(to1, LANES)] = jnp.where(left, 0.0, g).astype(BF16)
        return c

    pl.semaphore_signal(hint, inc=1, device_id=at_zh(-1))
    across(1).start()
    across(2).start()
    to_x(0)
    loads[3].wait()
    lax.fori_loop(0, SIDE, pad_down, 0)
    pl.semaphore_wait(hint, 1)
    across(3).start()
    lax.fori_loop(SIDE, 2 * SIDE, pad_down, 0)

    def arrived(c):
        for i in range(1, xs):
            over_x(c, i).wait_recv()
        own_out(c)
        if c == 0:
            wu[:, 64:128, width : 2 * width] = jnp.zeros((wu.shape[0], 64, width), BF16)
            wu[:, 0:64, 2 * width : 3 * width] = jnp.zeros((wu.shape[0], 64, width), BF16)
            for load in loads[:3]:
                load.wait()
            scaled = jnp.concatenate([jnp.where(p, weight, 0.0) for p in puts], axis=0)
            place[0] = scaled.astype(BF16)
            place[1] = (scaled - scaled.astype(BF16).astype(F32)).astype(BF16)

    def line(c, j, n):
        src, dst, to = (
            (a_up, ra_up, seg_up),
            (a_dn, ra_dn, seg_down),
            (b_up, rb_up, seg_up),
            (b_dn, rb_dn, seg_down),
            (b_far, rb_far, seg_far),
        )[n]
        return pltpu.make_async_remote_copy(
            src_ref=src.at[c, j],
            dst_ref=dst.at[c, j],
            send_sem=r_s.at[c, j, n],
            recv_sem=r_r.at[c, j, n],
            device_id={"seg": to},
        )

    def down_first(c, j):
        part = mm(hp[c], wd[zpeer[j]])
        own[c, j] = part[:, 256:384]
        if SUM_DIRECT[c]:
            b_far[c, j] = part[:, 0:128].astype(BF16)
            line(c, j, 4).start()
            b_up[c, j] = part[:, 384:512].astype(BF16)
            line(c, j, 2).start()
            b_dn[c, j] = part[:, 128:256].astype(BF16)
            line(c, j, 3).start()
            return
        a_up[c, j] = part[0:half, 0:128].astype(BF16)
        a_dn[c, j] = part[half:chunk, 0:128].astype(BF16)
        line(c, j, 0).start()
        line(c, j, 1).start()
        b_up[c, j, half:chunk] = part[half:chunk, 384:512].astype(BF16)
        b_dn[c, j, 0:half] = part[0:half, 128:256].astype(BF16)
        keep_up[c, j] = part[0:half, 384:512]
        keep_dn[c, j] = part[half:chunk, 128:256]

    def down_second(c, j):
        line(c, j, 0).wait_recv()
        b_up[c, j, 0:half] = (keep_up[c, j] + ra_up[c, j].astype(F32)).astype(BF16)
        line(c, j, 2).start()
        line(c, j, 1).wait_recv()
        b_dn[c, j, half:chunk] = (keep_dn[c, j] + ra_dn[c, j].astype(F32)).astype(BF16)
        line(c, j, 3).start()

    def gather_left(c, j):
        if j:
            zcopy(c, j).wait_send()
        for n in (0, 1, 4) if GATHER_DIRECT[c] else range(4):
            ycopy(c, j, n).wait_send()

    def zsum(c, j):
        return pltpu.make_async_remote_copy(
            src_ref=zs.at[c, j],
            dst_ref=zr.at[c, j],
            send_sem=zz_s.at[c, j],
            recv_sem=zz_r.at[c, j],
            device_id={"seg": zpeer[j] * SIDE + y},
        )

    def straight(j, i):
        to = (x + i) % xs
        return pltpu.make_async_remote_copy(
            src_ref=zs.at[0, j, pl.ds(to * PACK, PACK)],
            dst_ref=rb0.at[j, pl.ds(x * PACK, PACK)],
            send_sem=t0_s.at[j, i],
            recv_sem=t0_r.at[j, i],
            device_id={"expert": zh * xs + to, "seg": zpeer[j] * SIDE + y},
        )

    def down_third(c, j):
        line(c, j, 2).wait_recv()
        line(c, j, 3).wait_recv()
        gather_left(c, j)
        total = own[c, j] + rb_up[c, j].astype(F32) + rb_dn[c, j].astype(F32)
        if SUM_DIRECT[c]:
            line(c, j, 4).wait_recv()
            total += rb_far[c, j].astype(F32)
        if c == 0:
            zs[0, j] = total.astype(BF16)
            for i in range(j == 0, xs):
                straight(j, i).start()
            if j == 0:
                rb0[0, mine, :] = zs[0, 0, mine, :]
        elif j:
            zs[c, j] = total.astype(BF16)
            zsum(c, j).start()
        else:
            own[c, j] = total

    def home(c, i):
        to = (x + i) % xs
        return pltpu.make_async_remote_copy(
            src_ref=fb.at[c, pl.ds(to * PACK, PACK)],
            dst_ref=rb2.at[c, pl.ds(x * PACK, PACK)],
            send_sem=th_s.at[c, i],
            recv_sem=th_r.at[c, i],
            device_id={"expert": (zh + OFF[c]) % SIDE * xs + to},
        )

    def finish(c):
        total = own[c, 0]
        for j in range(1, SIDE):
            zsum(c, j).wait_recv()
            total += zr[c, j].astype(F32)
        fb[c] = total.astype(BF16)
        for i in range(xs):
            home(c, i).start()

    steps = (
        lambda c, j: arrived(c),
        z_out,
        y_pass,
        up_part,
        down_first,
        down_second,
        down_third,
        lambda c, j: finish(c),
        lambda c, j: to_x(c),
    )
    for step in ORDER:
        steps[step // 16](step % 16 // 4, step % 4)

    for c in range(SIDE):
        if c:
            across(c).wait_send()
        for i in range(1, xs):
            over_x(c, i).wait_send()
        for i in range(xs if c else 0):
            home(c, i).wait_send()
        for j in range(SIDE):
            if c == 0:
                for i in range(j == 0, xs):
                    straight(j, i).wait_send()
            elif j:
                zsum(c, j).wait_send()
            for n in (2, 3, 4) if SUM_DIRECT[c] else range(4):
                line(c, j, n).wait_send()
    for c in range(1, SIDE):
        for i in range(xs):
            home(c, i).wait_recv()
    total = jnp.zeros((chunk, LANES), F32)
    for j in range(SIDE):
        for i in range(j == 0, xs):
            straight(j, i).wait_recv()
        total += rb0[j].astype(F32)
    rb2[0] = total.astype(BF16)
    got = rb2[...].reshape(rows, LANES)
    mixed = mm(place[0], got) + mm(place[1], got)
    out_ref[:, 0:128] = mixed[0:tokens].astype(BF16)
    tail = mixed[tokens : 2 * tokens, 0:64] + mixed[2 * tokens : 3 * tokens, 64:128]
    out_ref[:, 128:192] = tail.astype(BF16)


def shards(experts, tokens, expert_ids, route_weight, w_up, w_down):
    segs = SIDE * SIDE
    xs = experts // SIDE
    chunk = xs * PACK
    half = chunk // 2
    width = w_up.shape[2]
    count, block = tokens.shape
    vm = pltpu.VMEM
    dma = pltpu.SemaphoreType.DMA
    each = (SIDE, SIDE)
    return pl.pallas_call(
        functools.partial(layer, experts),
        out_shape=jax.ShapeDtypeStruct(tokens.shape, BF16),
        in_specs=[pl.BlockSpec(memory_space=pl.ANY)] * 5,
        out_specs=pl.BlockSpec(memory_space=vm),
        scratch_shapes=[
            vm(tokens.shape, BF16),
            vm(expert_ids.shape[::-1], jnp.int32),
            vm(route_weight.shape[::-1], F32),
            vm((SIDE, chunk, LANES), BF16),
            vm((SIDE, chunk, LANES), BF16),
            vm((SIDE, segs, chunk, LANES), BF16),
            vm((segs, LANES, 3 * width), BF16),
            vm((width, segs * block), BF16),
            vm((SIDE, 3 * width, SIDE * LANES), BF16),
            vm((SIDE, chunk, 3 * width), F32),
            vm((SIDE, chunk, 3 * width), BF16),
            vm((2, 3 * count, SIDE * chunk), BF16),
            vm((*each, half, LANES), BF16),
            vm((*each, half, LANES), BF16),
            vm((*each, chunk, LANES), BF16),
            vm((*each, chunk, LANES), BF16),
            vm((*each, chunk, LANES), BF16),
            vm((*each, half, LANES), BF16),
            vm((*each, half, LANES), BF16),
            vm((*each, chunk, LANES), BF16),
            vm((*each, chunk, LANES), BF16),
            vm((*each, chunk, LANES), BF16),
            vm((*each, half, LANES), F32),
            vm((*each, half, LANES), F32),
            vm((*each, chunk, LANES), F32),
            vm((*each, chunk, LANES), BF16),
            vm((*each, chunk, LANES), BF16),
            vm((SIDE, chunk, LANES), BF16),
            vm((SIDE, chunk, LANES), BF16),
            vm((SIDE, chunk, LANES), BF16),
            dma((3,)),
            dma((4,)),
            pltpu.SemaphoreType.REGULAR,
            dma((SIDE, xs)),
            dma((SIDE, xs)),
            dma((SIDE,)),
            dma((SIDE,)),
            dma(each),
            dma(each),
            dma((*each, 5)),
            dma((*each, 5)),
            dma((*each, 5)),
            dma((*each, 5)),
            dma(each),
            dma(each),
            dma((SIDE, xs)),
            dma((SIDE, xs)),
            dma((SIDE, xs)),
            dma((SIDE, xs)),
        ],
        compiler_params=pltpu.CompilerParams(
            collective_id=0, has_side_effects=True, vmem_limit_bytes=56 * 2**20
        ),
    )(
        tokens,
        expert_ids.T,
        route_weight.T,
        w_up.reshape(segs, block, width),
        w_down.reshape(width, segs * block),
    )


def solution(mesh):
    placed = (
        P(("dp", "expert"), "seg"),
        P(("dp", "expert"), None),
        P(("dp", "expert"), None),
        P("expert", None, "seg"),
        P("expert", "seg", None),
    )
    return jax.shard_map(
        functools.partial(shards, mesh.shape["expert"]),
        mesh=mesh,
        in_specs=placed,
        out_specs=P(("dp", "expert"), "seg"),
        check_vma=False,
    )
```

```python
import functools

import jax
import jax.numpy as jnp
from jax import lax
from jax.experimental import pallas as pl
from jax.experimental.pallas import tpu as pltpu
from jax.sharding import PartitionSpec as P

CAP = 21
PACK = 32
LANES = 128
SIDE = 4
OFF = (0, 1, 3, 2)
GATHER_DIRECT = (1, 0, 0, 0)
SUM_DIRECT = (0, 0, 0, 1)
ORDER = (
    0, 132, 136, 17, 48, 4, 8, 18, 19, 140, 49, 36, 21, 40, 22, 50,
    23, 12, 25, 52, 51, 37, 26, 56, 38, 27, 39, 44, 29, 41, 53, 30,
    42, 54, 31, 43, 55, 69, 70, 45, 71, 68, 46, 60, 57, 58, 47, 59,
    85, 73, 86, 74, 87, 75, 84, 72, 61, 62, 63, 77, 101, 89, 78, 79,
    102, 90, 76, 65, 103, 91, 66, 67, 100, 88, 64, 109, 105, 110, 116, 111,
    106, 108, 81, 107, 82, 83, 104, 124, 80, 97, 98, 99, 120, 96,
)
F32 = jnp.float32
BF16 = jnp.bfloat16


def mm(a, b):
    return jnp.dot(a, b, preferred_element_type=F32)


def mm_t(a, b):
    return lax.dot_general(a, b, (((0,), (0,)), ((), ())), preferred_element_type=F32)


def layer(
    experts, tok_hbm, ids_hbm, rw_hbm, wup_ref, wdn_ref, out_ref,
    tok_ref, ids_ref, rw_ref, sbuf, mid, ag, wu, wraw, wd, acc, hp, place, a_up, a_dn, b_up, b_dn, b_far, ra_up, ra_dn, rb_up, rb_dn, rb_far,
    keep_up, keep_dn, own, zs, zr, fb, rb0, rb2,
    isem, wsem, hint, dx_s, dx_r, dz_s, dz_r, z_s, z_r, y_s, y_r, r_s, r_r, zz_s, zz_r, th_s, th_r, t0_s, t0_r,
):
    topk = ids_ref.shape[0]
    tokens = tok_ref.shape[0]
    xs = experts // SIDE
    chunk = xs * PACK
    half = chunk // 2
    rows = SIDE * chunk
    width = wup_ref.shape[2]
    e = lax.axis_index("expert")
    s = lax.axis_index("seg")
    zh, x = e // xs, e % xs
    zl, y = s // SIDE, s % SIDE
    up = (y + 1) % SIDE
    down = (y + SIDE - 1) % SIDE
    far = (y + 2) % SIDE
    zpeer = [zl, zl + 1 - 2 * (zl % 2), (zl + 2) % SIDE, SIDE - 1 - zl]
    seg_up, seg_down, seg_far = zl * SIDE + up, zl * SIDE + down, zl * SIDE + far

    def at_zh(off):
        return {"expert": (zh + SIDE + off) % SIDE * xs + x}

    def at_x(i):
        return {"expert": zh * xs + (x + i) % xs}

    small = [
        pltpu.make_async_copy(tok_hbm, tok_ref, isem.at[0]),
        pltpu.make_async_copy(ids_hbm, ids_ref, isem.at[1]),
        pltpu.make_async_copy(rw_hbm, rw_ref, isem.at[2]),
    ]
    for c in small:
        c.start()
    barrier = pltpu.get_barrier_semaphore()
    near = [at_zh(1), at_zh(-1)] + [at_x(i) for i in range(1, xs)]
    near += [{"seg": seg_up}, {"seg": seg_down}, {"seg": seg_far}]
    near += [{"seg": zpeer[j] * SIDE + y} for j in range(1, SIDE)]
    for to in near:
        pl.semaphore_signal(barrier, inc=1, device_id=to)

    loads = [
        pltpu.make_async_copy(wup_ref.at[:, 0:128, :], wu.at[:, :, 0:width], wsem.at[0]),
        pltpu.make_async_copy(wup_ref.at[:, 128:192, :], wu.at[:, 0:64, width : 2 * width], wsem.at[1]),
        pltpu.make_async_copy(wup_ref.at[:, 128:192, :], wu.at[:, 64:128, 2 * width : 3 * width], wsem.at[2]),
        pltpu.make_async_copy(wdn_ref, wraw, wsem.at[3]),
    ]
    for c in loads:
        c.start()

    for c in small:
        c.wait()
    table = jnp.concatenate([ids_ref[...].astype(F32), rw_ref[...]], axis=0).T
    ids, rw = table[:, 0:topk], table[:, topk : 2 * topk]
    norm = rw / jnp.sum(rw, axis=1, keepdims=True)
    lane = lax.broadcasted_iota(jnp.int32, (tokens, rows), 1)
    lane_c, lane_x, lane_r = lane // chunk, lane % chunk // PACK, lane % PACK
    lane_off = jnp.where(lane_c == 0, 0, jnp.where(lane_c == 1, 1, 5 - lane_c))
    lane_e = ((zh + SIDE - lane_off) % SIDE * xs + lane_x).astype(F32)
    weight = jnp.zeros((tokens, rows), F32)
    named = jnp.zeros((tokens, rows), F32)
    for k in range(topk):
        hit = ids[:, k : k + 1] == lane_e
        named = jnp.where(hit, 1.0, named)
        weight = jnp.where(hit, norm[:, k : k + 1], weight)
    earlier = lax.broadcasted_iota(jnp.int32, (tokens, tokens), 1) < lax.broadcasted_iota(
        jnp.int32, (tokens, tokens), 0
    )
    slot = mm(jnp.where(earlier, 1.0, 0.0).astype(BF16), named.astype(BF16)).astype(jnp.int32)
    main = lane_r < CAP
    puts = (main & (slot == lane_r), ~main & (slot == lane_r - CAP), ~main & (slot == lane_r - 10))
    tok = tok_ref[...]
    rest = tok[:, 128:192].astype(F32)
    blank = jnp.zeros((tokens, 64), F32)
    source = jnp.concatenate(
        [
            tok[:, 0:128],
            jnp.concatenate([rest, blank], axis=1).astype(BF16),
            jnp.concatenate([blank, rest], axis=1).astype(BF16),
        ],
        axis=0,
    )
    onehot = jnp.concatenate([jnp.where(p, named, 0.0) for p in puts], axis=0)
    sbuf[...] = mm_t(onehot.astype(BF16), source).astype(BF16).reshape(SIDE, chunk, LANES)

    pl.semaphore_wait(barrier, len(near))

    def across(c):
        return pltpu.make_async_remote_copy(
            src_ref=sbuf.at[c],
            dst_ref=mid.at[c],
            send_sem=dz_s.at[c],
            recv_sem=dz_r.at[c],
            device_id=at_zh(-OFF[c]),
        )

    def over_x(c, i):
        to = (x + i) % xs
        return pltpu.make_async_remote_copy(
            src_ref=(mid if c else sbuf).at[c, pl.ds(to * PACK, PACK)],
            dst_ref=ag.at[c, s, pl.ds(x * PACK, PACK)],
            send_sem=dx_s.at[c, i],
            recv_sem=dx_r.at[c, i],
            device_id=at_x(i),
        )

    mine = pl.ds(x * PACK, PACK)

    def to_x(c):
        if c:
            across(c).wait_recv()
        for i in range(1, xs):
            over_x(c, i).start()
        ag[c, s, mine, :] = (mid if c else sbuf)[c, mine, :]

    def zcopy(c, j):
        return pltpu.make_async_remote_copy(
            src_ref=ag.at[c, s],
            dst_ref=ag.at[c, s],
            send_sem=z_s.at[c, j],
            recv_sem=z_r.at[c, j],
            device_id={"seg": zpeer[j] * SIDE + y},
        )

    def z_arrival(c, j):
        g = zpeer[j] * SIDE + y
        return pltpu.make_async_remote_copy(
            src_ref=ag.at[c, g],
            dst_ref=ag.at[c, g],
            send_sem=z_s.at[c, j],
            recv_sem=z_r.at[c, j],
            device_id={"seg": g},
        )

    def ycopy(c, j, line):
        col, part, to = (
            (y, pl.ds(0, chunk), seg_up),
            (y, pl.ds(0, chunk), seg_down),
            (down, pl.ds(0, half), seg_up),
            (up, pl.ds(half, half), seg_down),
            (y, pl.ds(0, chunk), seg_far),
        )[line]
        g = zpeer[j] * SIDE + col
        return pltpu.make_async_remote_copy(
            src_ref=ag.at[c, g, part],
            dst_ref=ag.at[c, g, part],
            send_sem=y_s.at[c, j, line],
            recv_sem=y_r.at[c, j, line],
            device_id={"seg": to},
        )

    def y_arrival(c, j, line):
        col, part = (
            (down, pl.ds(0, chunk)),
            (up, pl.ds(0, chunk)),
            (far, pl.ds(0, half)),
            (far, pl.ds(half, half)),
            (far, pl.ds(0, chunk)),
        )[line]
        g = zpeer[j] * SIDE + col
        return pltpu.make_async_remote_copy(
            src_ref=ag.at[c, g, part],
            dst_ref=ag.at[c, g, part],
            send_sem=y_s.at[c, j, line],
            recv_sem=y_r.at[c, j, line],
            device_id={"seg": seg_up},
        )

    def y_send(c, j):
        ycopy(c, j, 0).start()
        ycopy(c, j, 1).start()
        if GATHER_DIRECT[c]:
            ycopy(c, j, 4).start()

    def own_out(c):
        for j in range(1, SIDE):
            zcopy(c, j).start()
        y_send(c, 0)

    def z_out(c, j):
        z_arrival(c, j).wait_recv()
        y_send(c, j)

    def y_pass(c, j):
        y_arrival(c, j, 0).wait_recv()
        ycopy(c, j, 2).start()
        y_arrival(c, j, 1).wait_recv()
        ycopy(c, j, 3).start()

    r = lax.broadcasted_iota(jnp.int32, (chunk, width), 0) % PACK

    summed = [0] * SIDE

    def up_part(c, j):
        for n in (0, 1, 4) if GATHER_DIRECT[c] else (2, 3):
            y_arrival(c, j, n).wait_recv()
        g = zpeer[j] * SIDE
        lhs = jnp.concatenate([ag[c, g + i] for i in range(SIDE)], axis=1)
        u = mm(lhs, wu[pl.ds(g, SIDE)].reshape(SIDE * LANES, 3 * width))
        if summed[c]:
            u += acc[c]
        summed[c] += 1
        if summed[c] < SIDE:
            acc[c] = u
            return
        v = u[:, 0:width] + jnp.where(
            r < 11,
            pltpu.roll(u[:, width : 2 * width], chunk - 21, 0),
            pltpu.roll(u[:, 2 * width : 3 * width], chunk - 10, 0),
        )
        h = jnp.where(r < CAP, v / (1.0 + jnp.exp(-v)), 0.0)
        hp[c, :, 0:width] = h.astype(BF16)
        hp[c, :, width : 2 * width] = jnp.where(r < CAP, 0.0, pltpu.roll(h, 21, 0)).astype(BF16)
        hp[c, :, 2 * width : 3 * width] = jnp.where(r < CAP, 0.0, pltpu.roll(h, 10, 0)).astype(BF16)

    left = lax.broadcasted_iota(jnp.int32, (width, LANES), 1) < 64

    def pad_down(i, c):
        z, q = i // 2, i % 2
        base = pl.multiple_of(i * 384, 128)
        a = wraw[:, pl.ds(base, 128)]
        b = wraw[:, pl.ds(base + 128, 128)].astype(F32)
        g = wraw[:, pl.ds(base + 256, 128)].astype(F32)
        b_turn, g_turn = pltpu.roll(b, 64, 1), pltpu.roll(g, 64, 1)
        to0 = pl.multiple_of((2 * q + 6 - y) % SIDE * LANES, LANES)
        to1 = pl.multiple_of((2 * q + 7 - y) % SIDE * LANES, LANES)
        wd[z, 0:width, pl.ds(to0, LANES)] = a
        wd[z, width : 2 * width, pl.ds(to0, LANES)] = jnp.where(left, b, 0.0).astype(BF16)
        wd[z, 2 * width : 3 * width, pl.ds(to0, LANES)] = jnp.where(left, 0.0, b_turn).astype(BF16)
        wd[z, 0:width, pl.ds(to1, LANES)] = jnp.where(left, b_turn, g_turn).astype(BF16)
        wd[z, width : 2 * width, pl.ds(to1, LANES)] = jnp.where(left, g_turn, 0.0).astype(BF16)
        wd[z, 2 * width : 3 * width, pl.ds(to1, LANES)] = jnp.where(left, 0.0, g).astype(BF16)
        return c

    pl.semaphore_signal(hint, inc=1, device_id=at_zh(-1))
    across(1).start()
    across(2).start()
    to_x(0)
    loads[3].wait()
    lax.fori_loop(0, SIDE, pad_down, 0)
    pl.semaphore_wait(hint, 1)
    across(3).start()
    lax.fori_loop(SIDE, 2 * SIDE, pad_down, 0)

    def arrived(c):
        for i in range(1, xs):
            over_x(c, i).wait_recv()
        own_out(c)
        if c == 0:
            wu[:, 64:128, width : 2 * width] = jnp.zeros((wu.shape[0], 64, width), BF16)
            wu[:, 0:64, 2 * width : 3 * width] = jnp.zeros((wu.shape[0], 64, width), BF16)
            for load in loads[:3]:
                load.wait()
            scaled = jnp.concatenate([jnp.where(p, weight, 0.0) for p in puts], axis=0)
            place[0] = scaled.astype(BF16)
            place[1] = (scaled - scaled.astype(BF16).astype(F32)).astype(BF16)

    def line(c, j, n):
        src, dst, to = (
            (a_up, ra_up, seg_up),
            (a_dn, ra_dn, seg_down),
            (b_up, rb_up, seg_up),
            (b_dn, rb_dn, seg_down),
            (b_far, rb_far, seg_far),
        )[n]
        return pltpu.make_async_remote_copy(
            src_ref=src.at[c, j],
            dst_ref=dst.at[c, j],
            send_sem=r_s.at[c, j, n],
            recv_sem=r_r.at[c, j, n],
            device_id={"seg": to},
        )

    def down_first(c, j):
        part = mm(hp[c], wd[zpeer[j]])
        own[c, j] = part[:, 256:384]
        if SUM_DIRECT[c]:
            b_far[c, j] = part[:, 0:128].astype(BF16)
            line(c, j, 4).start()
            b_up[c, j] = part[:, 384:512].astype(BF16)
            line(c, j, 2).start()
            b_dn[c, j] = part[:, 128:256].astype(BF16)
            line(c, j, 3).start()
            return
        a_up[c, j] = part[0:half, 0:128].astype(BF16)
        a_dn[c, j] = part[half:chunk, 0:128].astype(BF16)
        line(c, j, 0).start()
        line(c, j, 1).start()
        b_up[c, j, half:chunk] = part[half:chunk, 384:512].astype(BF16)
        b_dn[c, j, 0:half] = part[0:half, 128:256].astype(BF16)
        keep_up[c, j] = part[0:half, 384:512]
        keep_dn[c, j] = part[half:chunk, 128:256]

    def down_second(c, j):
        line(c, j, 0).wait_recv()
        b_up[c, j, 0:half] = (keep_up[c, j] + ra_up[c, j].astype(F32)).astype(BF16)
        line(c, j, 2).start()
        line(c, j, 1).wait_recv()
        b_dn[c, j, half:chunk] = (keep_dn[c, j] + ra_dn[c, j].astype(F32)).astype(BF16)
        line(c, j, 3).start()

    def gather_left(c, j):
        if j:
            zcopy(c, j).wait_send()
        for n in (0, 1, 4) if GATHER_DIRECT[c] else range(4):
            ycopy(c, j, n).wait_send()

    def zsum(c, j):
        return pltpu.make_async_remote_copy(
            src_ref=zs.at[c, j],
            dst_ref=zr.at[c, j],
            send_sem=zz_s.at[c, j],
            recv_sem=zz_r.at[c, j],
            device_id={"seg": zpeer[j] * SIDE + y},
        )

    def straight(j, i):
        to = (x + i) % xs
        return pltpu.make_async_remote_copy(
            src_ref=zs.at[0, j, pl.ds(to * PACK, PACK)],
            dst_ref=rb0.at[j, pl.ds(x * PACK, PACK)],
            send_sem=t0_s.at[j, i],
            recv_sem=t0_r.at[j, i],
            device_id={"expert": zh * xs + to, "seg": zpeer[j] * SIDE + y},
        )

    def down_third(c, j):
        line(c, j, 2).wait_recv()
        line(c, j, 3).wait_recv()
        gather_left(c, j)
        total = own[c, j] + rb_up[c, j].astype(F32) + rb_dn[c, j].astype(F32)
        if SUM_DIRECT[c]:
            line(c, j, 4).wait_recv()
            total += rb_far[c, j].astype(F32)
        if c == 0:
            zs[0, j] = total.astype(BF16)
            for i in range(j == 0, xs):
                straight(j, i).start()
            if j == 0:
                rb0[0, mine, :] = zs[0, 0, mine, :]
        elif j:
            zs[c, j] = total.astype(BF16)
            zsum(c, j).start()
        else:
            own[c, j] = total

    def home(c, i):
        to = (x + i) % xs
        return pltpu.make_async_remote_copy(
            src_ref=fb.at[c, pl.ds(to * PACK, PACK)],
            dst_ref=rb2.at[c, pl.ds(x * PACK, PACK)],
            send_sem=th_s.at[c, i],
            recv_sem=th_r.at[c, i],
            device_id={"expert": (zh + OFF[c]) % SIDE * xs + to},
        )

    def sums_left(c):
        if c:
            across(c).wait_send()
        for i in range(1, xs):
            over_x(c, i).wait_send()
        for j in range(SIDE):
            if c == 0:
                for i in range(j == 0, xs):
                    straight(j, i).wait_send()
            elif j:
                zsum(c, j).wait_send()
            for n in (2, 3, 4) if SUM_DIRECT[c] else range(4):
                line(c, j, n).wait_send()

    def finish(c):
        total = own[c, 0]
        for j in range(1, SIDE):
            zsum(c, j).wait_recv()
            total += zr[c, j].astype(F32)
        fb[c] = total.astype(BF16)
        for i in range(xs):
            home(c, i).start()
        sums_left(c)

    steps = (
        lambda c, j: arrived(c),
        z_out,
        y_pass,
        up_part,
        down_first,
        down_second,
        down_third,
        lambda c, j: finish(c),
        lambda c, j: to_x(c),
    )
    for step in ORDER:
        steps[step // 16](step % 16 // 4, step % 4)

    sums_left(0)
    for c in range(1, SIDE):
        for i in range(xs):
            home(c, i).wait_send()
    for c in range(1, SIDE):
        for i in range(xs):
            home(c, i).wait_recv()
    total = jnp.zeros((chunk, LANES), F32)
    for j in range(SIDE):
        for i in range(j == 0, xs):
            straight(j, i).wait_recv()
        total += rb0[j].astype(F32)
    rb2[0] = total.astype(BF16)
    got = rb2[...].reshape(rows, LANES)
    mixed = mm(place[0], got) + mm(place[1], got)
    out_ref[:, 0:128] = mixed[0:tokens].astype(BF16)
    tail = mixed[tokens : 2 * tokens, 0:64] + mixed[2 * tokens : 3 * tokens, 64:128]
    out_ref[:, 128:192] = tail.astype(BF16)


def shards(experts, tokens, expert_ids, route_weight, w_up, w_down):
    segs = SIDE * SIDE
    xs = experts // SIDE
    chunk = xs * PACK
    half = chunk // 2
    width = w_up.shape[2]
    count, block = tokens.shape
    vm = pltpu.VMEM
    dma = pltpu.SemaphoreType.DMA
    each = (SIDE, SIDE)
    return pl.pallas_call(
        functools.partial(layer, experts),
        out_shape=jax.ShapeDtypeStruct(tokens.shape, BF16),
        in_specs=[pl.BlockSpec(memory_space=pl.ANY)] * 5,
        out_specs=pl.BlockSpec(memory_space=vm),
        scratch_shapes=[
            vm(tokens.shape, BF16),
            vm(expert_ids.shape[::-1], jnp.int32),
            vm(route_weight.shape[::-1], F32),
            vm((SIDE, chunk, LANES), BF16),
            vm((SIDE, chunk, LANES), BF16),
            vm((SIDE, segs, chunk, LANES), BF16),
            vm((segs, LANES, 3 * width), BF16),
            vm((width, segs * block), BF16),
            vm((SIDE, 3 * width, SIDE * LANES), BF16),
            vm((SIDE, chunk, 3 * width), F32),
            vm((SIDE, chunk, 3 * width), BF16),
            vm((2, 3 * count, SIDE * chunk), BF16),
            vm((*each, half, LANES), BF16),
            vm((*each, half, LANES), BF16),
            vm((*each, chunk, LANES), BF16),
            vm((*each, chunk, LANES), BF16),
            vm((*each, chunk, LANES), BF16),
            vm((*each, half, LANES), BF16),
            vm((*each, half, LANES), BF16),
            vm((*each, chunk, LANES), BF16),
            vm((*each, chunk, LANES), BF16),
            vm((*each, chunk, LANES), BF16),
            vm((*each, half, LANES), F32),
            vm((*each, half, LANES), F32),
            vm((*each, chunk, LANES), F32),
            vm((*each, chunk, LANES), BF16),
            vm((*each, chunk, LANES), BF16),
            vm((SIDE, chunk, LANES), BF16),
            vm((SIDE, chunk, LANES), BF16),
            vm((SIDE, chunk, LANES), BF16),
            dma((3,)),
            dma((4,)),
            pltpu.SemaphoreType.REGULAR,
            dma((SIDE, xs)),
            dma((SIDE, xs)),
            dma((SIDE,)),
            dma((SIDE,)),
            dma(each),
            dma(each),
            dma((*each, 5)),
            dma((*each, 5)),
            dma((*each, 5)),
            dma((*each, 5)),
            dma(each),
            dma(each),
            dma((SIDE, xs)),
            dma((SIDE, xs)),
            dma((SIDE, xs)),
            dma((SIDE, xs)),
        ],
        compiler_params=pltpu.CompilerParams(
            collective_id=0, has_side_effects=True, vmem_limit_bytes=56 * 2**20
        ),
    )(
        tokens,
        expert_ids.T,
        route_weight.T,
        w_up.reshape(segs, block, width),
        w_down.reshape(width, segs * block),
    )


def solution(mesh):
    placed = (
        P(("dp", "expert"), "seg"),
        P(("dp", "expert"), None),
        P(("dp", "expert"), None),
        P("expert", None, "seg"),
        P("expert", "seg", None),
    )
    return jax.shard_map(
        functools.partial(shards, mesh.shape["expert"]),
        mesh=mesh,
        in_specs=placed,
        out_specs=P(("dp", "expert"), "seg"),
        check_vma=False,
    )
```
